32 devices in a mesh: page: 8 (over y, x, core), seq: 4 (over z).
Axes of the slice: x: 2, y: 2, z: 4, core: 2. Of those that a mesh axis runs over, the one named last changes fastest.
Arguments:
- tokens: bfloat16 [8, 2048, 1024], P('page', 'seq'), may hold values from -6 to 6
- memory: bfloat16 [8, 640, 1024], P('page', 'seq'), may hold values from -6 to 6
- cotangent: bfloat16 [8, 2048, 1024], P('page', 'seq'), may hold values from -6 to 6
- res_flag: int32 [8], P('page'), may hold values from 0 to 1
- ln_gain: bfloat16 [3, 1024], P(None, ('page', 'seq')), may hold values from 0.5 to 1.5
- ln_bias: bfloat16 [3, 1024], P(None, ('page', 'seq')), may hold values from -1 to 1
- self_in: bfloat16 [3, 1024, 1024], P(None, ('page', 'seq')), may hold values from -0.1875 to 0.1875
- self_out: bfloat16 [1024, 1024], P(('page', 'seq')), may hold values from -1.5 to 1.5
- cross_in: bfloat16 [3, 1024, 1024], P(None, ('page', 'seq')), may hold values from -0.1875 to 0.1875
- cross_out: bfloat16 [1024, 1024], P(('page', 'seq')), may hold values from -1 to 1
- ff_in: bfloat16 [1024, 4096], P(('page', 'seq')), may hold values from -0.1875 to 0.1875
- ff_out: bfloat16 [4096, 1024], P(('page', 'seq')), may hold values from -0.09375 to 0.09375
- proj_bias: bfloat16 [7, 1024], P(None, ('page', 'seq')), may hold values from -0.59765625 to 0.59765625
- ff_bias: bfloat16 [4096], P(('page', 'seq')), may hold values from -0.59765625 to 0.59765625
Outputs:
- layer_out: bfloat16 [8, 2048, 1024], P('page', 'seq')
- grad_tokens: float32 [8, 2048, 1024], P('page', 'seq')
- grad_memory: float32 [8, 640, 1024], P('page', 'seq')
- grad_ln_gain: float32 [3, 1024], P(None, ('page', 'seq'))
- grad_ln_bias: float32 [3, 1024], P(None, ('page', 'seq'))
- grad_self_in: float32 [3, 1024, 1024], P(None, ('page', 'seq'))
- grad_self_out: float32 [1024, 1024], P(('page', 'seq'))
- grad_cross_in: float32 [3, 1024, 1024], P(None, ('page', 'seq'))
- grad_cross_out: float32 [1024, 1024], P(('page', 'seq'))
- grad_ff_in: float32 [1024, 4096], P(('page', 'seq'))
- grad_ff_out: float32 [4096, 1024], P(('page', 'seq'))
- grad_proj_bias: float32 [7, 1024], P(None, ('page', 'seq'))
- grad_ff_bias: float32 [4096], P(('page', 'seq'))
The draws below stay inside these ranges and needn't reach their ends.
Inputs may be any that keep to these rules, and one draw needn't show every extreme that they name: A page with res_flag 1 has its first 588 memory rows valid, one with 0 its first 140; the other rows are padding.
All inputs are finite; a program needn't handle non-finite values.
Results may differ from the reference program's by a relative error of at most 0.023.
Values may be sent and summed in bfloat16 or wider, within the bound.
No kernel may reach another device: no remote copies, remote signals or barrier semaphores. Data moves between devices by JAX's collectives and lax.ppermute only.
A program may use at most 256 MiB of HBM per device.

```python
import jax
import jax.numpy as jnp
from jax import lax

D = 1024
HEADS = 16
HEAD_DIM = 64
FF = 4096
MEM = 640
VALID_HI = 588
VALID_LO = 140
PAGES = 8
LENGTH = 2048


def set_ends(values, stream_key, least, largest):
    index_at = [jax.random.randint(jax.random.fold_in(stream_key, axis), (), 0, length) for axis, length in enumerate(values.shape)]
    longest = values.shape.index(max(values.shape))
    next_to = index_at[:longest] + [(index_at[longest] + 1) % values.shape[longest]] + index_at[longest + 1:]
    return values.at[tuple(index_at)].set(least).at[tuple(next_to)].set(largest)


def levels(own_key, extent, shards, low, largest):
    level = 1.0
    for position, parts in shards:
        steps = jax.random.uniform(jax.random.fold_in(jax.random.fold_in(own_key, 6), position), (parts,), jnp.float32, low / len(shards), largest / len(shards))
        level = level * jnp.repeat(jnp.exp(steps), extent[position] // parts).reshape((-1,) + (1,) * (len(extent) - 1 - position))
    return level


def noise(stream_key, shape, width, bound, pieces=(), held_as=jnp.bfloat16):
    gain = levels(stream_key, shape, pieces, -0.22, 0.18) if pieces else 1.0
    array = jax.random.normal(stream_key, shape, jnp.float32) * width * gain
    return jnp.minimum(jnp.maximum(array, -bound), bound).astype(held_as)


def setup_inputs(seed: int = 0) -> dict:
    streams_of = jax.random.split(jax.random.key(seed), 15)
    tokens = noise(streams_of[0], (PAGES, LENGTH, D), 1.0, 6.0, ((0, 8), (1, 4)))
    memory = noise(streams_of[1], (PAGES, MEM, D), 1.0, 6.0, ((0, 8), (1, 4)))
    cotangent = noise(streams_of[2], (PAGES, LENGTH, D), 1.0, 6.0, ((0, 8), (1, 4)))
    res_flag = set_ends(jax.random.randint(streams_of[3], (PAGES,), 0, 2), jax.random.fold_in(streams_of[3], 1), 0, 1).astype(jnp.int32)
    ln_gain = jnp.clip(1.0 + 0.1 * jax.random.normal(streams_of[4], (3, D), jnp.float32), 0.5, 1.5).astype(jnp.bfloat16)
    ln_bias = noise(streams_of[5], (3, D), 0.2, 1.0, ((1, 32),))
    self_in = noise(streams_of[6], (3, D, D), D ** -0.5, 0.1875, ((1, 32),))
    self_out = noise(streams_of[7], (D, D), (D // 64) ** -0.5, 1.5, ((0, 32),))
    cross_in = noise(streams_of[8], (3, D, D), D ** -0.5, 0.1875, ((1, 32),))
    cross_out = noise(streams_of[9], (D, D), (D // 32) ** -0.5, 1.0, ((0, 32),))
    ff_in = noise(streams_of[10], (D, FF), D ** -0.5, 0.1875, ((0, 32),))
    ff_out = noise(streams_of[11], (FF, D), FF ** -0.5, 0.09375, ((0, 32),))
    proj_bias = noise(streams_of[12], (7, D), 0.1, 0.59765625, ((1, 32),))
    ff_bias = noise(streams_of[13], (FF,), 0.1, 0.59765625, ((0, 32),))
    return {"tokens": tokens, "memory": memory, "cotangent": cotangent, "res_flag": res_flag, "ln_gain": ln_gain, "ln_bias": ln_bias, "self_in": self_in, "self_out": self_out, "cross_in": cross_in, "cross_out": cross_out, "ff_in": ff_in, "ff_out": ff_out, "proj_bias": proj_bias, "ff_bias": ff_bias}


@jax.custom_vjp
def low(v):
    return lax.optimization_barrier(v.astype(jnp.bfloat16)).astype(jnp.float32)

@jax.custom_vjp
def low_back(v):
    return v

def low_keep(v):
    return (low(v), None)

def low_pass(kept, grad):
    return (grad,)

def back_keep(v):
    return (v, None)

def back_low(kept, grad):
    return (low(grad),)
low.defvjp(low_keep, low_pass)
low_back.defvjp(back_keep, back_low)
HIGHEST = lax.Precision.HIGHEST
NEGATIVE = -1e+30
EPSILON = 1e-05

def layer_norm(values, ln_scale, ln_shift):
    center_mean = lax.optimization_barrier(jnp.mean(values, axis=-1, keepdims=True))
    centered = values - center_mean
    variance = lax.optimization_barrier(jnp.mean(centered * centered, axis=-1, keepdims=True))
    return centered * lax.rsqrt(variance + EPSILON) * ln_scale + ln_shift

def matmul(left_rows, right_rows):
    return jnp.dot(left_rows, right_rows, precision=HIGHEST)

def attention(query_rows, key_rows, value_rows, key_valid, causal):
    row_total = query_rows.shape[0]
    block_rows = min(512, row_total)
    block_count = row_total // block_rows
    scaling = HEAD_DIM ** (-0.5)
    key_heads = key_rows.reshape(-1, HEADS, HEAD_DIM)
    value_heads = value_rows.reshape(-1, HEADS, HEAD_DIM)
    query_blocks = query_rows.reshape(block_count, block_rows, HEADS, HEAD_DIM)
    firsts = block_rows * jnp.arange(block_count, dtype=jnp.int32)
    key_places = jnp.arange(key_rows.shape[0], dtype=jnp.int32)

    def one_block(packed):
        query_part, first_row = packed
        scores = low_back(jnp.einsum('qhe,khe->hqk', query_part, key_heads, precision=HIGHEST) * scaling)
        allowed = jnp.broadcast_to(key_valid[None, :], (block_rows, key_places.shape[0]))
        if causal:
            places = first_row + jnp.arange(block_rows, dtype=jnp.int32)
            allowed = allowed & (key_places[None, :] <= places[:, None])
        scores = jnp.where(allowed[None], scores, NEGATIVE)
        attn_probs = low(jax.nn.softmax(scores, axis=-1))
        return jnp.einsum('hqk,khe->qhe', attn_probs, value_heads, precision=HIGHEST)
    result = lax.map(jax.checkpoint(one_block), (query_blocks, firsts))
    return result.reshape(row_total, HEADS * HEAD_DIM)

def page_layer(tokens, memory, valid_limit, params):
    ln_gain, ln_bias, self_in, self_out, cross_in, cross_out, ff_in, ff_out, proj_bias, ff_bias = params
    length_rows = tokens.shape[0]
    h_one = low(layer_norm(tokens, ln_gain[0], ln_bias[0]))
    q_self = low(low_back(matmul(h_one, self_in[0]) + proj_bias[0]))
    k_self = low(low_back(matmul(h_one, self_in[1])))
    v_self = low(low_back(matmul(h_one, self_in[2]) + proj_bias[1]))
    all_valid = jnp.ones((length_rows,), dtype=jnp.bool_)
    attended = low(low_back(attention(q_self, k_self, v_self, all_valid, True)))
    x_one = tokens + low_back(matmul(attended, self_out)) + proj_bias[2]
    h_two = low(layer_norm(x_one, ln_gain[1], ln_bias[1]))
    q_cross = low(low_back(matmul(h_two, cross_in[0]) + proj_bias[3]))
    k_cross = low(low_back(matmul(memory, cross_in[1])))
    v_cross = low(low_back(matmul(memory, cross_in[2]) + proj_bias[4]))
    mem_valid = jnp.arange(memory.shape[0], dtype=jnp.int32) < valid_limit
    attended_cross = low(low_back(attention(q_cross, k_cross, v_cross, mem_valid, False)))
    x_two = x_one + low_back(matmul(attended_cross, cross_out)) + proj_bias[5]
    h_three = low(layer_norm(x_two, ln_gain[2], ln_bias[2]))
    pre_act = low_back(matmul(h_three, ff_in) + ff_bias)
    act_rows = low(jax.nn.gelu(pre_act, approximate=False))
    return x_two + low_back(matmul(act_rows, ff_out)) + proj_bias[6]

def reference(tokens, memory, cotangent, res_flag, ln_gain, ln_bias, self_in, self_out, cross_in, cross_out, ff_in, ff_out, proj_bias, ff_bias):
    params = tuple((member.astype(jnp.float32) for member in (ln_gain, ln_bias, self_in, self_out, cross_in, cross_out, ff_in, ff_out, proj_bias, ff_bias)))
    limits = jnp.where(res_flag == 1, VALID_HI, VALID_LO).astype(jnp.int32)

    def forward(token_all, memory_all, weight_set):

        def one_page(packed):
            return page_layer(packed[0], packed[1], packed[2], weight_set)
        return lax.map(jax.checkpoint(one_page), (token_all, memory_all, limits))
    result, pullback = jax.vjp(forward, tokens.astype(jnp.float32), memory.astype(jnp.float32), params)
    grad_tokens, grad_memory, grad_list = pullback(cotangent.astype(jnp.float32))
    return (result.astype(jnp.bfloat16), grad_tokens, grad_memory, grad_list[0], grad_list[1], grad_list[2], grad_list[3], grad_list[4], grad_list[5], grad_list[6], grad_list[7], grad_list[8], grad_list[9])
```

```python
import functools

import jax
import jax.numpy as jnp
from jax import lax
from jax.experimental import pallas as pl
from jax.experimental.pallas import tpu as pltpu
from jax.sharding import PartitionSpec as P

HEADS = 16
HEAD_DIM = 64
VALID_HI = 588
VALID_LO = 140

NEGATIVE = -1e30
EPSILON = 1e-05
LOG2E = 1.4426950408889634
SCALING = HEAD_DIM ** (-0.5)
AXES = ("page", "seq")
F32 = jnp.float32
BF16 = jnp.bfloat16
NT = (((1,), (1,)), ((), ()))
NN = (((1,), (0,)), ((), ()))
TN = (((0,), (0,)), ((), ()))


def dot(a, b, dims=NN):
    return lax.dot_general(a, b, dims, preferred_element_type=F32)


def self_fwd_kernel(q_ref, kv_ref, o_ref, lse_ref, *, rows, width):
    i = pl.program_id(1)
    heads = width // HEAD_DIM
    queries = [q_ref[0, :, h * HEAD_DIM : (h + 1) * HEAD_DIM] for h in range(heads)]
    ones = jnp.ones((16, rows), BF16)

    def step(j, carry, diagonal):
        at = pl.ds(pl.multiple_of(j * rows, rows), rows)
        keys_all = kv_ref[0, at, width : 2 * width]
        values_t = kv_ref[0, at, 2 * width : 3 * width].T
        out = []
        for h in range(heads):
            run_max, acc = carry[h]
            lanes = slice(h * HEAD_DIM, (h + 1) * HEAD_DIM)
            scores = dot(keys_all[:, lanes], queries[h], NT) * (SCALING * LOG2E)
            if diagonal:
                place_k = lax.broadcasted_iota(jnp.int32, (rows, rows), 0)
                place_q = lax.broadcasted_iota(jnp.int32, (rows, rows), 1)
                scores = jnp.where(place_k <= place_q, scores, NEGATIVE)
            new_max = jnp.maximum(run_max, jnp.max(scores, axis=0, keepdims=True))
            probs = jnp.exp2(scores - new_max).astype(BF16)
            wide = jnp.concatenate([values_t[lanes], ones], axis=0)
            out.append((new_max, acc * jnp.exp2(run_max - new_max) + dot(wide, probs)))
        return tuple(out)

    start = tuple(
        (jnp.full((1, rows), NEGATIVE, F32), jnp.zeros((HEAD_DIM + 16, rows), F32))
        for _ in range(heads)
    )
    carry = lax.fori_loop(0, i, lambda j, c: step(j, c, False), start)
    carry = step(i, carry, True)
    outs = []
    for h in range(heads):
        run_max, acc = carry[h]
        total = acc[HEAD_DIM : HEAD_DIM + 1]
        outs.append(acc[:HEAD_DIM] / total)
        lse_ref[0, h] = run_max + jnp.log2(total)
    o_ref[0] = jnp.concatenate(outs, axis=0).T.astype(BF16)


def self_fwd(qkv, rows):
    pages, length, three = qkv.shape
    width = three // 3
    heads = width // HEAD_DIM
    blocks = length // rows
    cost = pages * heads * length * length * HEAD_DIM * 2
    return pl.pallas_call(
        functools.partial(self_fwd_kernel, rows=rows, width=width),
        grid=(pages, blocks),
        in_specs=[
            pl.BlockSpec((1, rows, three), lambda p, i: (p, i, 0)),
            pl.BlockSpec((1, length, three), lambda p, i: (p, 0, 0)),
        ],
        out_specs=[
            pl.BlockSpec((1, rows, width), lambda p, i: (p, i, 0)),
            pl.BlockSpec((1, heads, 1, rows), lambda p, i: (p, 0, 0, i)),
        ],
        out_shape=[
            jax.ShapeDtypeStruct((pages, length, width), BF16),
            jax.ShapeDtypeStruct((pages, heads, 1, length), F32),
        ],
        compiler_params=pltpu.CompilerParams(vmem_limit_bytes=48 * 1024 * 1024),
        cost_estimate=pl.CostEstimate(
            flops=2 * cost, bytes_accessed=8 * qkv.size, transcendentals=cost // 256
        ),
    )(qkv, qkv)


def self_bwd_kernel(q_ref, kv_ref, do_ref, o_ref, lse_ref, out_ref, dk_acc, dv_acc, *, rows, width):
    i = pl.program_id(1)
    heads = width // HEAD_DIM

    @pl.when(i == 0)
    def _():
        dk_acc[...] = jnp.zeros_like(dk_acc)
        dv_acc[...] = jnp.zeros_like(dv_acc)

    q_all = q_ref[0, :, :width]
    do_all = do_ref[0]
    prod = (do_all.astype(F32) * o_ref[0].astype(F32)).T
    per_head = [slice(h * HEAD_DIM, (h + 1) * HEAD_DIM) for h in range(heads)]
    deltas = [jnp.sum(prod[s], axis=0, keepdims=True) for s in per_head]

    def step(j, carry, diagonal):
        at = pl.ds(pl.multiple_of(j * rows, rows), rows)
        k_all = kv_ref[0, at, width : 2 * width]
        v_all = kv_ref[0, at, 2 * width : 3 * width]
        k_t = k_all.T
        new, dks, dvs = [], [], []
        for h in range(heads):
            s = per_head[h]
            scores = dot(k_all[:, s], q_all[:, s], NT) * (SCALING * LOG2E)
            probs = jnp.exp2(scores - lse_ref[0, h])
            if diagonal:
                place_k = lax.broadcasted_iota(jnp.int32, (rows, rows), 0)
                place_q = lax.broadcasted_iota(jnp.int32, (rows, rows), 1)
                probs = jnp.where(place_k <= place_q, probs, 0.0)
            d_probs = dot(v_all[:, s], do_all[:, s], NT)
            d_scores = (probs * (d_probs - deltas[h])).astype(BF16)
            dvs.append(dot(probs.astype(BF16), do_all[:, s]))
            dks.append(dot(d_scores, q_all[:, s]))
            new.append(carry[h] + dot(k_t[s], d_scores))
        dk_acc[at, :] += jnp.concatenate(dks, axis=1)
        dv_acc[at, :] += jnp.concatenate(dvs, axis=1)
        return tuple(new)

    start = tuple(jnp.zeros((HEAD_DIM, rows), F32) for _ in range(heads))
    carry = lax.fori_loop(0, i, lambda j, c: step(j, c, False), start)
    carry = step(i, carry, True)
    dq = (jnp.concatenate(carry, axis=0) * SCALING).T.astype(BF16)
    out_ref[0, pl.ds(pl.multiple_of(i * rows, rows), rows), :width] = dq

    @pl.when(i == pl.num_programs(1) - 1)
    def _():
        out_ref[0, :, width : 2 * width] = (dk_acc[...] * SCALING).astype(BF16)
        out_ref[0, :, 2 * width :] = dv_acc[...].astype(BF16)


def self_bwd(qkv, d_out, out, lse, rows):
    pages, length, three = qkv.shape
    width = three // 3
    heads = width // HEAD_DIM
    cost = pages * heads * length * length * HEAD_DIM * 5
    return pl.pallas_call(
        functools.partial(self_bwd_kernel, rows=rows, width=width),
        grid=(pages, length // rows),
        in_specs=[
            pl.BlockSpec((1, rows, three), lambda p, i: (p, i, 0)),
            pl.BlockSpec((1, length, three), lambda p, i: (p, 0, 0)),
            pl.BlockSpec((1, rows, width), lambda p, i: (p, i, 0)),
            pl.BlockSpec((1, rows, width), lambda p, i: (p, i, 0)),
            pl.BlockSpec((1, heads, 1, rows), lambda p, i: (p, 0, 0, i)),
        ],
        out_specs=pl.BlockSpec((1, length, three), lambda p, i: (p, 0, 0)),
        out_shape=jax.ShapeDtypeStruct((pages, length, three), BF16),
        scratch_shapes=[pltpu.VMEM((length, width), F32), pltpu.VMEM((length, width), F32)],
        compiler_params=pltpu.CompilerParams(vmem_limit_bytes=48 * 1024 * 1024),
        cost_estimate=pl.CostEstimate(
            flops=2 * cost, bytes_accessed=12 * qkv.size, transcendentals=cost // 640
        ),
    )(qkv, qkv, d_out, out, lse)


def cross_fwd_kernel(limit_ref, q_ref, k_ref, v_ref, o_ref, lse_ref):
    limit = limit_ref[0]
    rows, mem = q_ref.shape[0], k_ref.shape[0]
    valid = lax.broadcasted_iota(jnp.int32, (mem, rows), 0) < limit
    values_t = v_ref[...].T
    ones = jnp.ones((16, mem), BF16)
    outs = []
    for h in range(2):
        s = slice(h * HEAD_DIM, (h + 1) * HEAD_DIM)
        scores = dot(k_ref[:, s], q_ref[:, s], NT) * (SCALING * LOG2E)
        scores = jnp.where(valid, scores, NEGATIVE)
        top = jnp.max(scores, axis=0, keepdims=True)
        probs = jnp.exp2(scores - top).astype(BF16)
        acc = dot(jnp.concatenate([values_t[s], ones], axis=0), probs)
        total = acc[HEAD_DIM : HEAD_DIM + 1]
        outs.append(acc[:HEAD_DIM] / total)
        lse_ref[0, h : h + 1] = top + jnp.log2(total)
    o_ref[...] = jnp.concatenate(outs, axis=0).T.astype(BF16)


def cross_fwd(limit, q, kv):
    rows, width = q.shape
    mem = kv.shape[0]
    pairs = width // (2 * HEAD_DIM)
    wide = 2 * HEAD_DIM
    cost = width * rows * mem * 2
    return pl.pallas_call(
        cross_fwd_kernel,
        grid_spec=pltpu.PrefetchScalarGridSpec(
            num_scalar_prefetch=1,
            grid=(pairs,),
            in_specs=[
                pl.BlockSpec((rows, wide), lambda p, n: (0, p)),
                pl.BlockSpec((mem, wide), lambda p, n: (0, p)),
                pl.BlockSpec((mem, wide), lambda p, n: (0, p + pairs)),
            ],
            out_specs=[
                pl.BlockSpec((rows, wide), lambda p, n: (0, p)),
                pl.BlockSpec((1, 2, rows), lambda p, n: (p, 0, 0)),
            ],
        ),
        out_shape=[
            jax.ShapeDtypeStruct((rows, width), BF16),
            jax.ShapeDtypeStruct((pairs, 2, rows), F32),
        ],
        compiler_params=pltpu.CompilerParams(vmem_limit_bytes=48 * 1024 * 1024),
        cost_estimate=pl.CostEstimate(
            flops=2 * cost, bytes_accessed=4 * (q.size + kv.size), transcendentals=cost // 128
        ),
    )(limit, q, kv, kv)


def cross_bwd_kernel(limit_ref, q_ref, k_ref, v_ref, do_ref, o_ref, lse_ref, dq_ref, dk_ref, dv_ref):
    limit = limit_ref[0]
    rows, mem = q_ref.shape[0], k_ref.shape[0]
    valid = lax.broadcasted_iota(jnp.int32, (mem, rows), 0) < limit
    k_t = k_ref[...].T
    prod = (do_ref[...].astype(F32) * o_ref[...].astype(F32)).T
    dqs, dks, dvs = [], [], []
    for h in range(2):
        s = slice(h * HEAD_DIM, (h + 1) * HEAD_DIM)
        delta = jnp.sum(prod[s], axis=0, keepdims=True)
        scores = dot(k_ref[:, s], q_ref[:, s], NT) * (SCALING * LOG2E)
        scores = jnp.where(valid, scores, NEGATIVE)
        probs = jnp.exp2(scores - lse_ref[0, h : h + 1])
        d_probs = dot(v_ref[:, s], do_ref[:, s], NT)
        d_scores = (probs * (d_probs - delta)).astype(BF16)
        dvs.append(dot(probs.astype(BF16), do_ref[:, s]))
        dks.append(dot(d_scores, q_ref[:, s]))
        dqs.append(dot(k_t[s], d_scores))
    dq_ref[...] = (jnp.concatenate(dqs, axis=0) * SCALING).T.astype(BF16)
    dk_ref[...] = (jnp.concatenate(dks, axis=1) * SCALING).astype(BF16)
    dv_ref[...] = jnp.concatenate(dvs, axis=1).astype(BF16)


def cross_bwd(limit, q, kv, d_out, out, lse):
    rows, width = q.shape
    mem = kv.shape[0]
    pairs = width // (2 * HEAD_DIM)
    wide = 2 * HEAD_DIM
    cost = width * rows * mem * 5
    token_block = pl.BlockSpec((rows, wide), lambda p, n: (0, p))
    memory_block = pl.BlockSpec((mem, wide), lambda p, n: (0, p))
    return pl.pallas_call(
        cross_bwd_kernel,
        grid_spec=pltpu.PrefetchScalarGridSpec(
            num_scalar_prefetch=1,
            grid=(pairs,),
            in_specs=[
                token_block,
                memory_block,
                pl.BlockSpec((mem, wide), lambda p, n: (0, p + pairs)),
                token_block,
                token_block,
                pl.BlockSpec((1, 2, rows), lambda p, n: (p, 0, 0)),
            ],
            out_specs=[token_block, memory_block, memory_block],
        ),
        out_shape=[
            jax.ShapeDtypeStruct((rows, width), BF16),
            jax.ShapeDtypeStruct((mem, width), BF16),
            jax.ShapeDtypeStruct((mem, width), BF16),
        ],
        compiler_params=pltpu.CompilerParams(vmem_limit_bytes=48 * 1024 * 1024),
        cost_estimate=pl.CostEstimate(
            flops=2 * cost, bytes_accessed=6 * (q.size + kv.size), transcendentals=cost // 320
        ),
    )(limit, q, kv, kv, d_out, out, lse)


def gray(n):
    return n ^ (n >> 1)


class Net:
    def __init__(self, mesh):
        self.pages, self.seq = mesh.shape["page"], mesh.shape["seq"]
        self.chips = self.pages // 2
        page = lax.axis_index("page")
        self.core = lax.rem(page, 2)
        self.chip = lax.div(page, 2)
        self.z = lax.axis_index("seq")
        place = self.chip
        shift = 1
        while (self.chips - 1) >> shift:
            place = place ^ (self.chip >> shift)
            shift += 1
        self.place = place
        where = {gray(j): j for j in range(self.chips)}

        def index(chip, core, z):
            return (chip * 2 + core) * self.seq + z

        everyone = [
            (chip, core, z)
            for chip in range(self.chips)
            for core in range(2)
            for z in range(self.seq)
        ]
        self.pair_map = [(index(h, c, z), index(h, 1 - c, z)) for h, c, z in everyone]
        self.line_map = [
            [(index(h, c, z), index(h, c, (z + s) % self.seq)) for h, c, z in everyone]
            for s in range(self.seq)
        ]
        self.ring_map = {
            way: [
                (index(h, c, z), index(gray((where[h] + way) % self.chips), c, z))
                for h, c, z in everyone
            ]
            for way in (1, -1)
        }

    def sibling(self, value):
        return lax.ppermute(value, AXES, self.pair_map)

    def along(self, value, by):
        return lax.ppermute(value, AXES, self.line_map[by % self.seq])

    def around(self, value, way):
        return lax.ppermute(value, AXES, self.ring_map[way])

    def chip_at(self, by):
        j = lax.rem(self.place + by + self.chips, self.chips)
        return j ^ (j >> 1)

    def z_at(self, by):
        return lax.rem(self.z + by + self.seq, self.seq)


def put(buffer, piece, index, axis):
    return lax.dynamic_update_slice_in_dim(buffer, jnp.expand_dims(piece, axis), index, axis)


def pick(buffer, index, axis=0):
    return lax.dynamic_index_in_dim(buffer, index, axis, keepdims=False)


def line_gather(net, piece, axis):
    shape = piece.shape[:axis] + (net.seq,) + piece.shape[axis:]
    out = put(jnp.zeros(shape, piece.dtype), piece, net.z, axis)
    for s in range(1, net.seq):
        out = put(out, net.along(piece, s), net.z_at(-s), axis)
    return out


def ring_gather(net, piece):
    half = piece.shape[0] // 2
    out = put(jnp.zeros((net.chips,) + piece.shape, piece.dtype), piece, net.chip, 0)
    right, left = piece, piece
    for t in range(1, net.chips // 2):
        right, left = net.around(right, 1), net.around(left, -1)
        out = put(out, right, net.chip_at(-t), 0)
        out = put(out, left, net.chip_at(t), 0)
    far = net.chip_at(net.chips // 2)
    right, left = net.around(right[:half], 1), net.around(left[half:], -1)
    return put(out, jnp.concatenate([right, left], axis=0), far, 0)


def ring_scatter(net, parts):
    half = parts.shape[1] // 2
    steps = net.chips // 2
    far = pick(parts, net.chip_at(steps))
    right, left = net.around(far[:half], 1), net.around(far[half:], -1)
    for t in range(1, steps):
        k = steps - t
        mine = pick(parts, net.chip_at(k))
        if t == 1:
            first = mine[:half].astype(F32) + right.astype(F32)
            sent = jnp.concatenate([first.astype(BF16), mine[half:]], axis=0)
        else:
            sent = (mine.astype(F32) + right.astype(F32)).astype(BF16)
        mine = pick(parts, net.chip_at(-k))
        if t == 1:
            first = mine[half:].astype(F32) + left.astype(F32)
            back = jnp.concatenate([mine[:half], first.astype(BF16)], axis=0)
        else:
            back = (mine.astype(F32) + left.astype(F32)).astype(BF16)
        right, left = net.around(sent, 1), net.around(back, -1)
    return pick(parts, net.chip).astype(F32) + right.astype(F32) + left.astype(F32)


def line_scatter(net, parts, axis):
    low = parts.astype(BF16)
    total = pick(parts, net.z, axis).astype(F32)
    for s in range(1, net.seq):
        total += net.along(pick(low, net.z_at(s), axis), s).astype(F32)
    return total


def own_first(net, value):
    return pick(value, net.core), pick(value, 1 - net.core)


def by_core(net, own, other):
    return jnp.where(net.core == 0, jnp.stack([own, other]), jnp.stack([other, own]))


def gather_columns(net, shard):
    own, other = own_first(net, jnp.moveaxis(shard, 1, 0))
    piece = by_core(net, own, net.sibling(other))
    full = ring_gather(net, line_gather(net, piece, 1))
    return full.reshape(-1, full.shape[-1])


def gather_rows(net, shard):
    full = ring_gather(net, line_gather(net, shard, 0))
    return full.reshape(-1, full.shape[-1])


def scatter_columns(net, grad, rows):
    parts = grad.reshape(net.chips, 2, net.seq, rows, grad.shape[-1])
    mine = line_scatter(net, ring_scatter(net, parts), 1)
    own, other = own_first(net, mine)
    return jnp.moveaxis(by_core(net, own, net.sibling(other)), 0, 1)


def scatter_rows(net, grad, rows):
    parts = grad.reshape(net.chips, net.seq, rows, grad.shape[-1])
    return line_scatter(net, ring_scatter(net, parts), 0)


def norm_parts(values):
    centered = values - jnp.mean(values, axis=-1, keepdims=True)
    scale = lax.rsqrt(jnp.mean(centered * centered, axis=-1, keepdims=True) + EPSILON)
    return centered * scale, scale


def layer_norm(values, gain, shift):
    return (norm_parts(values)[0] * gain + shift).astype(BF16)


def norm_back(values, gain, upstream):
    normed, scale = norm_parts(values)
    scaled = upstream * gain
    mean_g = jnp.mean(scaled, axis=-1, keepdims=True)
    mean_gn = jnp.mean(scaled * normed, axis=-1, keepdims=True)
    grad = (scaled - mean_g - normed * mean_gn) * scale
    return grad, jnp.sum(upstream * normed, axis=0), jnp.sum(upstream, axis=0)


def column_sum(values):
    return jnp.sum(values.astype(F32), axis=0)


def on_device(
    tokens,
    memory,
    cotangent,
    res_flag,
    ln_gain,
    ln_bias,
    self_in,
    self_out,
    cross_in,
    cross_out,
    ff_in,
    ff_out,
    proj_bias,
    ff_bias,
    *,
    mesh,
):
    net = Net(mesh)
    core, z = net.core, net.z
    rows, width = tokens.shape[1], tokens.shape[2]
    seq, chips, pages = net.seq, net.chips, net.pages
    shard = self_in.shape[1]
    hidden = ff_in.shape[1]
    ff_shard = ff_out.shape[0]
    lanes = width // (2 * seq)
    half = width // 2
    tok, mem, cot = tokens[0], memory[0], cotangent[0]

    flag = jnp.broadcast_to(res_flag.astype(BF16)[:, None], (1, shard))
    small = jnp.concatenate(
        [ln_gain, ln_bias, proj_bias, flag, ff_bias.reshape(ff_shard // shard, shard)], axis=0
    )
    small = lax.all_gather(small, AXES, axis=0)
    vectors = jnp.moveaxis(small[:, :13], 0, 1).reshape(13, width).astype(F32)
    gain, shift, bias = vectors[0:3], vectors[3:6], vectors[6:13]
    flags = small[:, 13, 0].reshape(pages, seq)[:, 0].astype(F32)
    up_bias = small[:, 14:].reshape(chips, 2, seq * ff_shard)
    up_bias = pick(up_bias, core, 1).reshape(hidden // 2).astype(F32)
    page = lax.axis_index("page")

    def limit_of(which):
        return jnp.where(pick(flags, which) > 0.5, VALID_HI, VALID_LO).astype(jnp.int32).reshape(1)

    limit_own, limit_other = limit_of(page), limit_of(page ^ 1)

    def halves(vector):
        return pick(vector.reshape(pages // 2, 2, width // pages), core, 1).reshape(half)

    def column_halves(weight):
        lead, columns = weight.shape[:-1], weight.shape[-1]
        split = weight.reshape(lead + (pages // 2, 2, columns // pages))
        return jnp.moveaxis(split, -2, -3).reshape(lead + (2, columns // 2))

    def join_halves(weight):
        lead, columns = weight.shape[:-2], weight.shape[-1] * 2
        split = weight.reshape(lead + (2, pages // 2, columns // pages))
        return jnp.moveaxis(split, -3, -2).reshape(lead + (columns,))

    blocks = self_in.reshape(3, shard, seq, 2, lanes).transpose(3, 2, 1, 0, 4)
    blocks = blocks.reshape(2, seq, shard, 3 * lanes)
    own, other = own_first(net, blocks)
    blocks = by_core(net, own, net.sibling(other))
    piece = jnp.zeros_like(blocks)
    piece = put(piece, pick(blocks, z, 1), z, 1)
    for s in range(1, seq):
        piece = put(piece, net.along(pick(blocks, net.z_at(s), 1), s), net.z_at(-s), 1)
    w_qkv = ring_gather(net, piece).reshape(width, 3 * lanes)
    first = (2 * z + core) * lanes
    b_qkv = jnp.concatenate(
        [
            lax.dynamic_slice_in_dim(bias[0], first, lanes),
            jnp.zeros((lanes,), F32),
            lax.dynamic_slice_in_dim(bias[1], first, lanes),
        ]
    )

    h_all = jnp.zeros((2, seq, rows, width), BF16)
    qkv = jnp.zeros((2, seq, rows, 3 * lanes), BF16)
    passing = tok
    h_one = None
    for t in range(seq):
        if t:
            passing = net.along(passing, 1)
        both = jnp.stack([passing, net.sibling(passing)])
        h = layer_norm(both.astype(F32), gain[0], shift[0])
        h_all = put(h_all, h, net.z_at(-t), 1)
        part = dot(h.reshape(2 * rows, width), w_qkv) + b_qkv
        qkv = put(qkv, part.astype(BF16).reshape(2, rows, 3 * lanes), net.z_at(-t), 1)
    h_all = h_all.reshape(2 * seq * rows, width)
    qkv = qkv.reshape(2, seq * rows, 3 * lanes)

    w_outs = gather_rows(net, jnp.concatenate([self_out, cross_out], axis=1))
    w_self_out, w_cross_out = w_outs[:, :width], w_outs[:, width:]
    cross_halves = column_halves(cross_in)
    cross_halves = cross_halves.transpose(1, 2, 0, 3).reshape(shard, 2, 3 * half)
    w_cross = gather_columns(net, cross_halves)
    w_cross_q, w_cross_kv = w_cross[:, :half], w_cross[:, half:]
    w_up = gather_columns(net, column_halves(ff_in))
    w_down = gather_rows(net, ff_out)
    cot_two = jnp.concatenate([cot, net.sibling(cot)], axis=0)

    mem_page = line_gather(net, mem, 0).reshape(-1, width)
    mem_all = jnp.concatenate([mem_page, net.sibling(mem_page)], axis=0)
    mem_rows = mem_page.shape[0]
    b_kv = jnp.concatenate([jnp.zeros((half,), F32), halves(bias[4])])
    kv_cross = (dot(mem_all, w_cross_kv) + b_kv).astype(BF16)
    kv_own, kv_other = kv_cross[:mem_rows], kv_cross[mem_rows:]

    att_rows = min(512, rows)
    o_self, lse_self = self_fwd(qkv, att_rows)

    def to_tokens(value):
        blocks = value.reshape(2, seq, rows, lanes)
        out = jnp.zeros((2, rows, seq, lanes), BF16)
        out = put(out, pick(blocks, z, 1), z, 2)
        for s in range(1, seq):
            out = put(out, net.along(pick(blocks, net.z_at(s), 1), s), net.z_at(-s), 2)
        return out.reshape(2 * rows, half)

    def to_heads(value):
        blocks = value.reshape(2, rows, seq, lanes)
        out = jnp.zeros((2, seq, rows, lanes), BF16)
        out = put(out, pick(blocks, z, 2), z, 1)
        for s in range(1, seq):
            out = put(out, net.along(pick(blocks, net.z_at(s), 2), s), net.z_at(-s), 1)
        return out.reshape(2, seq * rows, lanes)

    def summed(rows_two, weight, dims=NN):
        sent = dot(rows_two[rows:], weight, dims).astype(BF16)
        back = net.sibling(sent)
        return dot(rows_two[:rows], weight, dims) + back.astype(F32)

    def both_pages(value):
        return jnp.concatenate([value, net.sibling(value)], axis=0)

    attended = to_tokens(o_self)
    x_in = tok.astype(F32)
    x_one = x_in + summed(attended, w_self_out) + bias[2]

    h_two = both_pages(layer_norm(x_one, gain[1], shift[1]))
    q_cross = (dot(h_two, w_cross_q) + halves(bias[3])).astype(BF16)
    oc_own, lse_own = cross_fwd(limit_own, q_cross[:rows], kv_own)
    oc_other, lse_other = cross_fwd(limit_other, q_cross[rows:], kv_other)
    o_cross = jnp.concatenate([oc_own, oc_other], axis=0)
    x_two = x_one + summed(o_cross, w_cross_out) + bias[5]

    h_three = both_pages(layer_norm(x_two, gain[2], shift[2]))
    pre_act = dot(h_three, w_up) + up_bias
    cdf = 0.5 + 0.5 * lax.erf(pre_act * (0.5**0.5))
    act = (pre_act * cdf).astype(BF16)
    layer_rows = (x_two + summed(act, w_down) + bias[6]).astype(BF16)

    slope = cdf + pre_act * (jnp.exp(-0.5 * pre_act * pre_act) * 0.3989422804014327)
    g_pre = (dot(cot_two, w_down, NT) * slope).astype(BF16)
    grad_down = dot(act, cot_two, TN).astype(BF16)
    grad_up = dot(h_three, g_pre, TN).astype(BF16)
    sum_down = scatter_rows(net, grad_down, ff_shard)
    sum_up = join_halves(scatter_columns(net, grad_up, shard))
    cot_wide = cot.astype(F32)
    back, d_gain2, d_shift2 = norm_back(x_two, gain[2], summed(g_pre, w_up, NT))
    g_two = cot_wide + back

    g_cross = both_pages(g_two.astype(BF16))
    grad_cross_out = dot(o_cross, g_cross, TN).astype(BF16)
    d_oc = dot(g_cross, w_cross_out, NT).astype(BF16)
    dq_own, dk_own, dv_own = cross_bwd(
        limit_own, q_cross[:rows], kv_own, d_oc[:rows], oc_own, lse_own
    )
    dq_other, dk_other, dv_other = cross_bwd(
        limit_other, q_cross[rows:], kv_other, d_oc[rows:], oc_other, lse_other
    )
    dq_cross = jnp.concatenate([dq_own, dq_other], axis=0)
    dkv_own = jnp.concatenate([dk_own, dv_own], axis=1)
    dkv_other = jnp.concatenate([dk_other, dv_other], axis=1)
    dkv_cross = jnp.concatenate([dkv_own, dkv_other], axis=0)
    grad_cross = jnp.concatenate(
        [dot(h_two, dq_cross, TN).astype(BF16), dot(mem_all, dkv_cross, TN).astype(BF16)], axis=1
    )
    sum_cross = scatter_columns(net, grad_cross, shard)
    sum_cross = sum_cross.reshape(shard, 2, 3, half).transpose(2, 0, 1, 3)
    sum_cross = join_halves(sum_cross)
    mem_sent = dot(dkv_other, w_cross_kv, NT).astype(BF16)
    mem_grad = dot(dkv_own, w_cross_kv, NT) + net.sibling(mem_sent).astype(F32)
    grad_memory = line_scatter(net, mem_grad.reshape(seq, -1, width), 0)
    back, d_gain1, d_shift1 = norm_back(x_one, gain[1], summed(dq_cross, w_cross_q, NT))
    g_one = g_two + back

    g_self = both_pages(g_one.astype(BF16))
    grad_self_out = dot(attended, g_self, TN).astype(BF16)
    sum_outs = scatter_rows(net, jnp.concatenate([grad_self_out, grad_cross_out], axis=1), shard)
    d_os = to_heads(dot(g_self, w_self_out, NT).astype(BF16))
    d_qkv = self_bwd(qkv, d_os, o_self, lse_self, att_rows)
    other_h = dot(d_qkv[1], w_qkv, NT).astype(BF16)
    d_h = dot(d_qkv[0], w_qkv, NT) + net.sibling(other_h).astype(F32)
    d_h = line_scatter(net, d_h.reshape(seq, rows, width), 0)
    flat = d_qkv.reshape(2 * seq * rows, 3 * lanes)
    grad_qkv = dot(h_all, flat, TN).astype(BF16)
    parts = ring_scatter(net, grad_qkv.reshape(chips, 2, seq * shard, 3 * lanes))
    parts = parts.astype(BF16).reshape(2, seq, shard, 3 * lanes)
    piece = jnp.zeros_like(parts)
    piece = put(piece, pick(parts, z, 1), z, 1)
    for s in range(1, seq):
        piece = put(piece, net.along(pick(parts, net.z_at(s), 1), s), net.z_at(-s), 1)
    own, other = own_first(net, piece)
    piece = by_core(net, own, net.sibling(other))
    sum_self = piece.reshape(2, seq, shard, 3, lanes).transpose(3, 2, 1, 0, 4)
    sum_self = sum_self.reshape(3, shard, width).astype(F32)
    back, d_gain0, d_shift0 = norm_back(x_in, gain[0], d_h)
    token_grad = g_one + back

    def spread(vector):
        split = vector.reshape(pages // 2, 1, width // pages)
        here = jnp.arange(2)[None, :, None] == core
        return jnp.where(here, split, 0.0).reshape(width)

    def spread_heads(vector):
        return lax.dynamic_update_slice_in_dim(jnp.zeros((width,), F32), vector, first, 0)

    sums_qkv = column_sum(flat)
    up_sum = column_sum(g_pre).reshape(chips, 1, seq * ff_shard)
    up_sum = jnp.where(jnp.arange(2)[None, :, None] == core, up_sum, 0.0)
    vectors = jnp.stack(
        [
            d_gain0,
            d_gain1,
            d_gain2,
            d_shift0,
            d_shift1,
            d_shift2,
            spread_heads(sums_qkv[:lanes]),
            spread_heads(sums_qkv[2 * lanes :]),
            column_sum(g_one),
            spread(column_sum(dq_cross)),
            spread(column_sum(dkv_cross[:, half:])),
            column_sum(g_two),
            column_sum(cot_wide),
        ]
    )
    vectors = jnp.moveaxis(vectors.reshape(13, pages * seq, shard), 0, 1)
    packed = jnp.concatenate(
        [vectors.reshape(pages * seq, 13 * shard), up_sum.reshape(pages * seq, ff_shard)], axis=1
    )
    packed = lax.psum_scatter(packed, AXES, scatter_dimension=0, tiled=True)[0]
    vectors = packed[: 13 * shard].reshape(13, shard)
    return (
        layer_rows[None],
        token_grad[None],
        grad_memory[None],
        vectors[0:3],
        vectors[3:6],
        sum_self,
        sum_outs[:, :width],
        sum_cross,
        sum_outs[:, width:],
        sum_up,
        sum_down,
        vectors[6:13],
        packed[13 * shard :],
    )


def solution(mesh):
    weight = P(AXES, None)
    return jax.shard_map(
        functools.partial(on_device, mesh=mesh),
        mesh=mesh,
        in_specs=(
            P("page", "seq", None),
            P("page", "seq", None),
            P("page", "seq", None),
            P("page"),
            P(None, AXES),
            P(None, AXES),
            P(None, AXES, None),
            weight,
            P(None, AXES, None),
            weight,
            weight,
            weight,
            P(None, AXES),
            P(AXES),
        ),
        out_specs=(
            P("page", "seq", None),
            P("page", "seq", None),
            P("page", "seq", None),
            P(None, AXES),
            P(None, AXES),
            P(None, AXES, None),
            weight,
            P(None, AXES, None),
            weight,
            weight,
            weight,
            P(None, AXES),
            P(AXES),
        ),
        check_vma=False,
    )
```

```python
import functools

import jax
import jax.numpy as jnp
from jax import lax
from jax.experimental import pallas as pl
from jax.experimental.pallas import tpu as pltpu
from jax.sharding import PartitionSpec as P

HEADS = 16
HEAD_DIM = 64
VALID_HI = 588
VALID_LO = 140

NEGATIVE = -1e30
EPSILON = 1e-05
LOG2E = 1.4426950408889634
SCALING = HEAD_DIM ** (-0.5)
AXES = ("page", "seq")
F32 = jnp.float32
BF16 = jnp.bfloat16
NT = (((1,), (1,)), ((), ()))
NN = (((1,), (0,)), ((), ()))
TN = (((0,), (0,)), ((), ()))


def dot(a, b, dims=NN):
    return lax.dot_general(a, b, dims, preferred_element_type=F32)


def project_kernel(spot_ref, x_ref, gain_ref, shift_ref, w_ref, b_ref, h_in, qkv_in, h_ref, qkv_ref):
    del spot_ref, h_in, qkv_in
    x = x_ref[...].astype(F32)
    centered = x - jnp.mean(x, axis=-1, keepdims=True)
    scale = lax.rsqrt(jnp.mean(centered * centered, axis=-1, keepdims=True) + EPSILON)
    h = (centered * scale * gain_ref[...] + shift_ref[...]).astype(BF16)
    h_ref[0, 0] = h
    qkv_ref[0, 0] = (dot(h, w_ref[...]) + b_ref[...]).astype(BF16)


def project(spot, x, gain, shift, w_qkv, b_qkv, h_all, qkv):
    rows, width = x.shape
    wide = w_qkv.shape[1]
    block = min(256, rows)
    whole = lambda shape: pl.BlockSpec(shape, lambda i, n: (0, 0))
    return pl.pallas_call(
        project_kernel,
        grid_spec=pltpu.PrefetchScalarGridSpec(
            num_scalar_prefetch=1,
            grid=(rows // block,),
            in_specs=[
                pl.BlockSpec((block, width), lambda i, n: (i, 0)),
                whole((1, width)),
                whole((1, width)),
                whole((width, wide)),
                whole((1, wide)),
                pl.BlockSpec(memory_space=pl.ANY),
                pl.BlockSpec(memory_space=pl.ANY),
            ],
            out_specs=[
                pl.BlockSpec((1, 1, block, width), lambda i, n: (n[0], n[1], i, 0)),
                pl.BlockSpec((1, 1, block, wide), lambda i, n: (n[0], n[1], i, 0)),
            ],
        ),
        out_shape=[
            jax.ShapeDtypeStruct(h_all.shape, BF16),
            jax.ShapeDtypeStruct(qkv.shape, BF16),
        ],
        input_output_aliases={6: 0, 7: 1},
        compiler_params=pltpu.CompilerParams(vmem_limit_bytes=32 * 1024 * 1024),
        cost_estimate=pl.CostEstimate(
            flops=2 * rows * width * wide, bytes_accessed=4 * rows * width, transcendentals=0
        ),
    )(spot, x, gain[None], shift[None], w_qkv, b_qkv[None], h_all, qkv)


def self_fwd_kernel(order_ref, q_ref, kv_ref, o_ref, lse_ref, *, rows, width):
    del order_ref
    i = pl.program_id(1)
    heads = width // HEAD_DIM
    queries = [q_ref[0, :, h * HEAD_DIM : (h + 1) * HEAD_DIM] for h in range(heads)]
    ones = jnp.ones((16, rows), BF16)

    def step(j, carry, diagonal):
        at = pl.ds(pl.multiple_of(j * rows, rows), rows)
        keys_all = kv_ref[0, at, width : 2 * width]
        values_t = kv_ref[0, at, 2 * width : 3 * width].T
        out = []
        for h in range(heads):
            run_max, acc = carry[h]
            lanes = slice(h * HEAD_DIM, (h + 1) * HEAD_DIM)
            scores = dot(keys_all[:, lanes], queries[h], NT) * (SCALING * LOG2E)
            if diagonal:
                place_k = lax.broadcasted_iota(jnp.int32, (rows, rows), 0)
                place_q = lax.broadcasted_iota(jnp.int32, (rows, rows), 1)
                scores = jnp.where(place_k <= place_q, scores, NEGATIVE)
            new_max = jnp.maximum(run_max, jnp.max(scores, axis=0, keepdims=True))
            probs = jnp.exp2(scores - new_max).astype(BF16)
            wide = jnp.concatenate([values_t[lanes], ones], axis=0)
            out.append((new_max, acc * jnp.exp2(run_max - new_max) + dot(wide, probs)))
        return tuple(out)

    start = tuple(
        (jnp.full((1, rows), NEGATIVE, F32), jnp.zeros((HEAD_DIM + 16, rows), F32))
        for _ in range(heads)
    )
    carry = lax.fori_loop(0, i, lambda j, c: step(j, c, False), start)
    carry = step(i, carry, True)
    outs = []
    for h in range(heads):
        run_max, acc = carry[h]
        total = acc[HEAD_DIM : HEAD_DIM + 1]
        outs.append(acc[:HEAD_DIM] / total)
        lse_ref[0, h] = run_max + jnp.log2(total)
    o_ref[0] = jnp.concatenate(outs, axis=0).T.astype(BF16)


def self_fwd(order, qkv, rows, page):
    length, three = qkv.shape[1:]
    width = three // 3
    heads = width // HEAD_DIM
    cost = heads * length * length * HEAD_DIM * 2
    return pl.pallas_call(
        functools.partial(self_fwd_kernel, rows=rows, width=width),
        grid=(1, length // rows),
        in_specs=[
            pl.BlockSpec(memory_space=pltpu.SMEM),
            pl.BlockSpec((1, rows, three), lambda p, i: (page, i, 0)),
            pl.BlockSpec((1, length, three), lambda p, i: (page, 0, 0)),
        ],
        out_specs=[
            pl.BlockSpec((1, rows, width), lambda p, i: (0, i, 0)),
            pl.BlockSpec((1, heads, 1, rows), lambda p, i: (0, 0, 0, i)),
        ],
        out_shape=[
            jax.ShapeDtypeStruct((1, length, width), BF16),
            jax.ShapeDtypeStruct((1, heads, 1, length), F32),
        ],
        compiler_params=pltpu.CompilerParams(vmem_limit_bytes=48 * 1024 * 1024),
        cost_estimate=pl.CostEstimate(
            flops=2 * cost, bytes_accessed=4 * qkv.size, transcendentals=cost // 256
        ),
    )(order, qkv, qkv)


def self_bwd_kernel(q_ref, kv_ref, do_ref, o_ref, lse_ref, out_ref, dk_acc, dv_acc, *, rows, width):
    i = pl.program_id(1)
    heads = width // HEAD_DIM

    @pl.when(i == 0)
    def _():
        dk_acc[...] = jnp.zeros_like(dk_acc)
        dv_acc[...] = jnp.zeros_like(dv_acc)

    q_all = q_ref[0, :, :width]
    do_all = do_ref[0]
    prod = (do_all.astype(F32) * o_ref[0].astype(F32)).T
    per_head = [slice(h * HEAD_DIM, (h + 1) * HEAD_DIM) for h in range(heads)]
    deltas = [jnp.sum(prod[s], axis=0, keepdims=True) for s in per_head]

    def step(j, carry, diagonal):
        at = pl.ds(pl.multiple_of(j * rows, rows), rows)
        k_all = kv_ref[0, at, width : 2 * width]
        v_all = kv_ref[0, at, 2 * width : 3 * width]
        k_t = k_all.T
        new, dks, dvs = [], [], []
        for h in range(heads):
            s = per_head[h]
            scores = dot(k_all[:, s], q_all[:, s], NT) * (SCALING * LOG2E)
            probs = jnp.exp2(scores - lse_ref[0, h])
            if diagonal:
                place_k = lax.broadcasted_iota(jnp.int32, (rows, rows), 0)
                place_q = lax.broadcasted_iota(jnp.int32, (rows, rows), 1)
                probs = jnp.where(place_k <= place_q, probs, 0.0)
            d_probs = dot(v_all[:, s], do_all[:, s], NT)
            d_scores = (probs * (d_probs - deltas[h])).astype(BF16)
            dvs.append(dot(probs.astype(BF16), do_all[:, s]))
            dks.append(dot(d_scores, q_all[:, s]))
            new.append(carry[h] + dot(k_t[s], d_scores))
        dk_acc[at, :] += jnp.concatenate(dks, axis=1)
        dv_acc[at, :] += jnp.concatenate(dvs, axis=1)
        return tuple(new)

    start = tuple(jnp.zeros((HEAD_DIM, rows), F32) for _ in range(heads))
    carry = lax.fori_loop(0, i, lambda j, c: step(j, c, False), start)
    carry = step(i, carry, True)
    dq = (jnp.concatenate(carry, axis=0) * SCALING).T.astype(BF16)
    out_ref[0, pl.ds(pl.multiple_of(i * rows, rows), rows), :width] = dq

    @pl.when(i == pl.num_programs(1) - 1)
    def _():
        out_ref[0, :, width : 2 * width] = (dk_acc[...] * SCALING).astype(BF16)
        out_ref[0, :, 2 * width :] = dv_acc[...].astype(BF16)


def self_bwd(qkv, d_out, out, lse, rows, page):
    length, three = qkv.shape[1:]
    width = three // 3
    heads = width // HEAD_DIM
    cost = heads * length * length * HEAD_DIM * 5
    return pl.pallas_call(
        functools.partial(self_bwd_kernel, rows=rows, width=width),
        grid=(1, length // rows),
        in_specs=[
            pl.BlockSpec((1, rows, three), lambda p, i: (page, i, 0)),
            pl.BlockSpec((1, length, three), lambda p, i: (page, 0, 0)),
            pl.BlockSpec((1, rows, width), lambda p, i: (page, i, 0)),
            pl.BlockSpec((1, rows, width), lambda p, i: (0, i, 0)),
            pl.BlockSpec((1, heads, 1, rows), lambda p, i: (0, 0, 0, i)),
        ],
        out_specs=pl.BlockSpec((1, length, three), lambda p, i: (0, 0, 0)),
        out_shape=jax.ShapeDtypeStruct((1, length, three), BF16),
        scratch_shapes=[pltpu.VMEM((length, width), F32), pltpu.VMEM((length, width), F32)],
        compiler_params=pltpu.CompilerParams(vmem_limit_bytes=48 * 1024 * 1024),
        cost_estimate=pl.CostEstimate(
            flops=2 * cost, bytes_accessed=6 * qkv.size, transcendentals=cost // 640
        ),
    )(qkv, qkv, d_out, out, lse)


def cross_fwd_kernel(limit_ref, q_ref, k_ref, v_ref, o_ref, lse_ref):
    limit = limit_ref[0]
    rows, mem = q_ref.shape[0], k_ref.shape[0]
    valid = lax.broadcasted_iota(jnp.int32, (mem, rows), 0) < limit
    values_t = v_ref[...].T
    ones = jnp.ones((16, mem), BF16)
    outs = []
    for h in range(2):
        s = slice(h * HEAD_DIM, (h + 1) * HEAD_DIM)
        scores = dot(k_ref[:, s], q_ref[:, s], NT) * (SCALING * LOG2E)
        scores = jnp.where(valid, scores, NEGATIVE)
        top = jnp.max(scores, axis=0, keepdims=True)
        probs = jnp.exp2(scores - top).astype(BF16)
        acc = dot(jnp.concatenate([values_t[s], ones], axis=0), probs)
        total = acc[HEAD_DIM : HEAD_DIM + 1]
        outs.append(acc[:HEAD_DIM] / total)
        lse_ref[0, h : h + 1] = top + jnp.log2(total)
    o_ref[...] = jnp.concatenate(outs, axis=0).T.astype(BF16)


def cross_fwd(limit, q, kv):
    rows, width = q.shape
    mem = kv.shape[0]
    pairs = width // (2 * HEAD_DIM)
    wide = 2 * HEAD_DIM
    cost = width * rows * mem * 2
    return pl.pallas_call(
        cross_fwd_kernel,
        grid_spec=pltpu.PrefetchScalarGridSpec(
            num_scalar_prefetch=1,
            grid=(pairs,),
            in_specs=[
                pl.BlockSpec((rows, wide), lambda p, n: (0, p)),
                pl.BlockSpec((mem, wide), lambda p, n: (0, p)),
                pl.BlockSpec((mem, wide), lambda p, n: (0, p + pairs)),
            ],
            out_specs=[
                pl.BlockSpec((rows, wide), lambda p, n: (0, p)),
                pl.BlockSpec((1, 2, rows), lambda p, n: (p, 0, 0)),
            ],
        ),
        out_shape=[
            jax.ShapeDtypeStruct((rows, width), BF16),
            jax.ShapeDtypeStruct((pairs, 2, rows), F32),
        ],
        compiler_params=pltpu.CompilerParams(vmem_limit_bytes=48 * 1024 * 1024),
        cost_estimate=pl.CostEstimate(
            flops=2 * cost, bytes_accessed=4 * (q.size + kv.size), transcendentals=cost // 128
        ),
    )(limit, q, kv, kv)


def cross_bwd_kernel(limit_ref, q_ref, k_ref, v_ref, do_ref, o_ref, lse_ref, dq_ref, dk_ref, dv_ref):
    limit = limit_ref[0]
    rows, mem = q_ref.shape[0], k_ref.shape[0]
    valid = lax.broadcasted_iota(jnp.int32, (mem, rows), 0) < limit
    k_t = k_ref[...].T
    prod = (do_ref[...].astype(F32) * o_ref[...].astype(F32)).T
    dqs, dks, dvs = [], [], []
    for h in range(2):
        s = slice(h * HEAD_DIM, (h + 1) * HEAD_DIM)
        delta = jnp.sum(prod[s], axis=0, keepdims=True)
        scores = dot(k_ref[:, s], q_ref[:, s], NT) * (SCALING * LOG2E)
        scores = jnp.where(valid, scores, NEGATIVE)
        probs = jnp.exp2(scores - lse_ref[0, h : h + 1])
        d_probs = dot(v_ref[:, s], do_ref[:, s], NT)
        d_scores = (probs * (d_probs - delta)).astype(BF16)
        dvs.append(dot(probs.astype(BF16), do_ref[:, s]))
        dks.append(dot(d_scores, q_ref[:, s]))
        dqs.append(dot(k_t[s], d_scores))
    dq_ref[...] = (jnp.concatenate(dqs, axis=0) * SCALING).T.astype(BF16)
    dk_ref[...] = (jnp.concatenate(dks, axis=1) * SCALING).astype(BF16)
    dv_ref[...] = jnp.concatenate(dvs, axis=1).astype(BF16)


def cross_bwd(limit, q, kv, d_out, out, lse):
    rows, width = q.shape
    mem = kv.shape[0]
    pairs = width // (2 * HEAD_DIM)
    wide = 2 * HEAD_DIM
    cost = width * rows * mem * 5
    token_block = pl.BlockSpec((rows, wide), lambda p, n: (0, p))
    memory_block = pl.BlockSpec((mem, wide), lambda p, n: (0, p))
    return pl.pallas_call(
        cross_bwd_kernel,
        grid_spec=pltpu.PrefetchScalarGridSpec(
            num_scalar_prefetch=1,
            grid=(pairs,),
            in_specs=[
                token_block,
                memory_block,
                pl.BlockSpec((mem, wide), lambda p, n: (0, p + pairs)),
                token_block,
                token_block,
                pl.BlockSpec((1, 2, rows), lambda p, n: (p, 0, 0)),
            ],
            out_specs=[token_block, memory_block, memory_block],
        ),
        out_shape=[
            jax.ShapeDtypeStruct((rows, width), BF16),
            jax.ShapeDtypeStruct((mem, width), BF16),
            jax.ShapeDtypeStruct((mem, width), BF16),
        ],
        compiler_params=pltpu.CompilerParams(vmem_limit_bytes=48 * 1024 * 1024),
        cost_estimate=pl.CostEstimate(
            flops=2 * cost, bytes_accessed=6 * (q.size + kv.size), transcendentals=cost // 320
        ),
    )(limit, q, kv, kv, d_out, out, lse)


def gray(n):
    return n ^ (n >> 1)


class Net:
    def __init__(self, mesh):
        self.pages, self.seq = mesh.shape["page"], mesh.shape["seq"]
        self.chips = self.pages // 2
        page = lax.axis_index("page")
        self.core = lax.rem(page, 2)
        self.chip = lax.div(page, 2)
        self.z = lax.axis_index("seq")
        place = self.chip
        shift = 1
        while (self.chips - 1) >> shift:
            place = place ^ (self.chip >> shift)
            shift += 1
        self.place = place
        where = {gray(j): j for j in range(self.chips)}

        def index(chip, core, z):
            return (chip * 2 + core) * self.seq + z

        everyone = [
            (chip, core, z)
            for chip in range(self.chips)
            for core in range(2)
            for z in range(self.seq)
        ]
        self.planes = [
            [index(chip, core, z) for chip in range(self.chips)]
            for core in range(2)
            for z in range(self.seq)
        ]
        self.pair_map = [(index(h, c, z), index(h, 1 - c, z)) for h, c, z in everyone]
        self.line_map = [
            [(index(h, c, z), index(h, c, (z + s) % self.seq)) for h, c, z in everyone]
            for s in range(self.seq)
        ]
        self.ring_map = {
            way: [
                (index(h, c, z), index(gray((where[h] + way) % self.chips), c, z))
                for h, c, z in everyone
            ]
            for way in (1, -1)
        }

    def sibling(self, value):
        return lax.ppermute(value, AXES, self.pair_map)

    def along(self, value, by):
        return lax.ppermute(value, AXES, self.line_map[by % self.seq])

    def around(self, value, way):
        return lax.ppermute(value, AXES, self.ring_map[way])

    def chip_at(self, by):
        j = lax.rem(self.place + by + self.chips, self.chips)
        return j ^ (j >> 1)

    def z_at(self, by):
        return lax.rem(self.z + by + self.seq, self.seq)


def put(buffer, piece, index, axis):
    return lax.dynamic_update_slice_in_dim(buffer, jnp.expand_dims(piece, axis), index, axis)


def pick(buffer, index, axis=0):
    return lax.dynamic_index_in_dim(buffer, index, axis, keepdims=False)


def line_pieces(net, piece):
    yield 0, piece
    right, left = piece, piece
    for t in range(1, net.seq // 2 + 1):
        right = net.along(right, 1)
        yield -t, right
        if t <= (net.seq - 1) // 2:
            left = net.along(left, -1)
            yield t, left


def line_gather(net, piece, axis):
    out = jnp.zeros(piece.shape[:axis] + (net.seq,) + piece.shape[axis:], piece.dtype)
    for by, got in line_pieces(net, piece):
        out = put(out, got, net.z_at(by), axis)
    return out


def line_gather_held(net, piece, axis, *others):
    out = put(jnp.zeros(piece.shape[:axis] + (net.seq,) + piece.shape[axis:], piece.dtype), piece, net.z, axis)
    for s in range(1, net.seq):
        out = put(out, after(net.along(piece, s), *others), net.z_at(-s), axis)
    return out


def ring_gather(net, piece):
    half = piece.shape[0] // 2
    out = put(jnp.zeros((net.chips,) + piece.shape, piece.dtype), piece, net.chip, 0)
    right, left = piece, piece
    for t in range(1, net.chips // 2):
        right, left = net.around(right, 1), net.around(left, -1)
        out = put(out, right, net.chip_at(-t), 0)
        out = put(out, left, net.chip_at(t), 0)
    far = net.chip_at(net.chips // 2)
    right, left = net.around(right[:half], 1), net.around(left[half:], -1)
    return put(out, jnp.concatenate([right, left], axis=0), far, 0)


def ring_scatter(net, parts):
    half = parts.shape[1] // 2
    steps = net.chips // 2
    far = pick(parts, net.chip_at(steps))
    right, left = net.around(far[:half], 1), net.around(far[half:], -1)
    for t in range(1, steps):
        k = steps - t
        mine = pick(parts, net.chip_at(k))
        if t == 1:
            first = mine[:half].astype(F32) + right.astype(F32)
            sent = jnp.concatenate([first.astype(BF16), mine[half:]], axis=0)
        else:
            sent = (mine.astype(F32) + right.astype(F32)).astype(BF16)
        mine = pick(parts, net.chip_at(-k))
        if t == 1:
            first = mine[half:].astype(F32) + left.astype(F32)
            back = jnp.concatenate([mine[:half], first.astype(BF16)], axis=0)
        else:
            back = (mine.astype(F32) + left.astype(F32)).astype(BF16)
        right, left = net.around(sent, 1), net.around(back, -1)
    return pick(parts, net.chip).astype(F32) + right.astype(F32) + left.astype(F32)


def line_scatter(net, parts, axis):
    low = parts.astype(BF16)
    sent = [pick(low, net.z_at(s), axis) for s in range(1, net.seq)]
    got = [net.along(value, s + 1) for s, value in enumerate(sent)]
    return pick(parts, net.z, axis).astype(F32) + sum(value.astype(F32) for value in got)


def own_first(net, value):
    return pick(value, net.core), pick(value, 1 - net.core)


def by_core(net, own, other):
    return jnp.where(net.core == 0, jnp.stack([own, other]), jnp.stack([other, own]))


def plane_gather(net, piece):
    return lax.all_gather(piece, AXES, axis=0, axis_index_groups=net.planes)


def plane_scatter(net, parts):
    flat = parts.reshape(-1, parts.shape[-1])
    mine = lax.psum_scatter(
        flat, AXES, scatter_dimension=0, axis_index_groups=net.planes, tiled=True
    )
    return mine.reshape(parts.shape[1:])


def seq_scatter(parts):
    flat = parts.reshape(-1, parts.shape[-1])
    mine = lax.psum_scatter(flat, "seq", scatter_dimension=0, tiled=True)
    return mine.reshape(parts.shape[1:]).astype(F32)


def after(value, *others):
    for other in others:
        element = lax.optimization_barrier(other)[(0,) * other.ndim].astype(F32)
        value = value + jnp.minimum(jnp.abs(element), 0.0).astype(value.dtype)
    return value


def scatter_columns(net, grad, rows):
    parts = grad.reshape(net.chips, 2, net.seq, rows, grad.shape[-1])
    mine = line_scatter(net, plane_scatter(net, parts), 1)
    own, other = own_first(net, mine)
    return jnp.moveaxis(by_core(net, own, net.sibling(other)), 0, 1)


def scatter_rows(net, grad, rows):
    parts = grad.reshape(net.chips, net.seq, rows, grad.shape[-1])
    return line_scatter(net, plane_scatter(net, parts), 0)


def line_two_way_scatter(net, parts):
    total = pick(parts, net.z)
    for way, far in ((1, net.seq // 2), (-1, (net.seq - 1) // 2)):
        got = None
        for by in range(far, 0, -1):
            mine = pick(parts, net.z_at(way * by))
            sent = (mine if got is None else mine + got).astype(BF16)
            got = net.along(sent, way).astype(F32)
        if got is not None:
            total += got
    return total


def norm_parts(values):
    centered = values - jnp.mean(values, axis=-1, keepdims=True)
    scale = lax.rsqrt(jnp.mean(centered * centered, axis=-1, keepdims=True) + EPSILON)
    return centered * scale, scale


def layer_norm(values, gain, shift):
    return (norm_parts(values)[0] * gain + shift).astype(BF16)


def norm_back(values, gain, upstream):
    normed, scale = norm_parts(values)
    scaled = upstream * gain
    mean_g = jnp.mean(scaled, axis=-1, keepdims=True)
    mean_gn = jnp.mean(scaled * normed, axis=-1, keepdims=True)
    grad = (scaled - mean_g - normed * mean_gn) * scale
    return grad, jnp.sum(upstream * normed, axis=0), jnp.sum(upstream, axis=0)


def column_sum(values):
    return jnp.sum(values.astype(F32), axis=0)


def on_device(
    tokens,
    memory,
    cotangent,
    res_flag,
    ln_gain,
    ln_bias,
    self_in,
    self_out,
    cross_in,
    cross_out,
    ff_in,
    ff_out,
    proj_bias,
    ff_bias,
    *,
    mesh,
):
    net = Net(mesh)
    core, z = net.core, net.z
    rows, width = tokens.shape[1], tokens.shape[2]
    seq, chips, pages = net.seq, net.chips, net.pages
    shard = self_in.shape[1]
    hidden = ff_in.shape[1]
    ff_shard = ff_out.shape[0]
    lanes = width // (2 * seq)
    half = width // 2
    tok, mem, cot = tokens[0], memory[0], cotangent[0]

    def halves(vector):
        return pick(vector.reshape(pages // 2, 2, width // pages), core, 1).reshape(half)

    def column_halves(weight):
        lead, columns = weight.shape[:-1], weight.shape[-1]
        split = weight.reshape(lead + (pages // 2, 2, columns // pages))
        return jnp.moveaxis(split, -2, -3).reshape(lead + (2, columns // 2))

    def join_halves(weight):
        lead, columns = weight.shape[:-2], weight.shape[-1] * 2
        split = weight.reshape(lead + (2, pages // 2, columns // pages))
        return jnp.moveaxis(split, -3, -2).reshape(lead + (columns,))

    side = 128
    small = jnp.concatenate(
        [
            ln_gain.T,
            ln_bias.T,
            proj_bias.T,
            jnp.broadcast_to(res_flag.astype(BF16)[:, None], (shard, 1)),
            ff_bias.reshape(shard, ff_shard // shard),
        ],
        axis=1,
    )
    small = jnp.pad(small, ((0, 0), (0, side - small.shape[1])))
    blocks = self_in.reshape(3, shard, seq, 2, lanes).transpose(3, 2, 1, 0, 4)
    blocks = blocks.reshape(2, seq, shard, 3 * lanes)
    small = jnp.broadcast_to(small, (2, seq, shard, side))
    blocks = jnp.concatenate([blocks, small], axis=3)
    own, other = own_first(net, blocks)
    blocks = by_core(net, own, net.sibling(other))
    piece = jnp.zeros_like(blocks)
    piece = put(piece, pick(blocks, z, 1), z, 1)
    for s in range(1, seq):
        piece = put(piece, net.along(pick(blocks, net.z_at(s), 1), s), net.z_at(-s), 1)
    qkv_line = piece
    w_wide = ring_gather(net, piece).reshape(width, 3 * lanes + side)
    w_qkv = w_wide[:, : 3 * lanes]
    small = w_wide[:, 3 * lanes :].astype(F32)
    vectors = small[:, :13].T
    gain, shift, bias = vectors[0:3], vectors[3:6], vectors[6:13]
    flags = small[:, 13].reshape(pages, seq * shard)[:, 0]
    up_bias = small[:, 14 : 14 + ff_shard // shard].reshape(chips, 2, seq * ff_shard)
    up_bias = pick(up_bias, core, 1).reshape(hidden // 2)
    page = lax.axis_index("page")

    def limit_of(which):
        return jnp.where(pick(flags, which) > 0.5, VALID_HI, VALID_LO).astype(jnp.int32).reshape(1)

    limit_own, limit_other = limit_of(page), limit_of(page ^ 1)

    limit_own, limit_other = limit_of(page), limit_of(page ^ 1)
    first = (2 * z + core) * lanes
    b_qkv = jnp.concatenate(
        [
            lax.dynamic_slice_in_dim(bias[0], first, lanes),
            jnp.zeros((lanes,), F32),
            lax.dynamic_slice_in_dim(bias[1], first, lanes),
        ]
    )

    cross_halves = column_halves(cross_in).transpose(2, 1, 0, 3).reshape(2, shard, 3 * half)
    column_parts = jnp.concatenate([cross_halves, column_halves(ff_in).transpose(1, 0, 2)], axis=2)
    own, other = own_first(net, column_parts)
    column_parts = by_core(net, own, net.sibling(other))
    cross_parts, up_parts = column_parts[:, :, : 3 * half], column_parts[:, :, 3 * half :]
    bundle = jnp.concatenate([cross_parts[0], cross_parts[1], self_out, cross_out], axis=1)
    bundle_line = line_gather(net, after(bundle, qkv_line), 0)
    bundle = plane_gather(net, bundle_line)

    def rows_of(at, columns):
        two = [bundle[..., c * 3 * half + at : c * 3 * half + at + columns] for c in range(2)]
        return jnp.stack(two, axis=1).reshape(width, columns)

    w_cross_q, w_cross_kv = rows_of(0, half), rows_of(half, width)
    w_self_out = bundle[..., 6 * half : 6 * half + width].reshape(half, width)
    w_cross_out = bundle[..., 6 * half + width :].reshape(half, width)
    h_all = jnp.zeros((2, seq, rows, width), BF16)
    qkv = jnp.zeros((2, seq, rows, 3 * lanes), BF16)
    right = left = passing = after(tok, qkv_line)
    for t in range(seq // 2 + 1):
        if t == 1:
            own_qkv = qkv
        if t == 2:
            right = after(right, own_qkv)
        ways = [(0, passing)]
        if t:
            right = passing = net.along(right, 1)
            ways = [(-t, right)]
            if t <= (seq - 1) // 2:
                left = net.along(left, -1)
                ways.append((t, left))
        for by, value in ways:
            for page_at, x in ((core, value), (1 - core, net.sibling(value))):
                spot = jnp.stack([page_at, net.z_at(by)]).astype(jnp.int32)
                h_all, qkv = project(spot, x, gain[0], shift[0], w_qkv, b_qkv, h_all, qkv)
    h_all = h_all.reshape(2 * seq * rows, width)
    qkv = qkv.reshape(2, seq * rows, 3 * lanes)

    cot_two = jnp.concatenate([cot, net.sibling(cot)], axis=0)

    att_rows = min(512, rows)
    def to_tokens(value):
        blocks = value.reshape(seq, rows, lanes)
        sent = [pick(blocks, net.z_at(-s)) for s in range(1, seq)]
        got = [net.along(value, -s - 1) for s, value in enumerate(sent)]
        return jnp.concatenate([pick(blocks, z)] + got, axis=1)

    def to_heads(value):
        blocks = by_core(net, value[:rows], value[rows:])
        out = put(jnp.zeros((2, seq, rows, lanes), BF16), blocks[..., :lanes], z, 1)
        for s in range(1, seq):
            got = net.along(blocks[..., s * lanes : (s + 1) * lanes], s)
            out = put(out, got, net.z_at(-s), 1)
        return out.reshape(2, seq * rows, lanes)

    def turned(weight, by):
        twice = jnp.concatenate([weight, weight], axis=0)
        return lax.dynamic_slice_in_dim(twice, by * lanes, half, axis=0)

    o_self, lse_self, attended = [], [], []
    order = jnp.zeros((1,), jnp.int32)
    for k in range(2):
        order = after(order, o_self[0]) if k else order
        out, lse = self_fwd(order, qkv, att_rows, k)
        o_self.append(out)
        lse_self.append(lse)
        attended.append(to_tokens(out[0]))
    attended = jnp.concatenate(own_first(net, jnp.stack(attended)), axis=0)
    up_line = line_gather_held(net, after(up_parts, passing), 1, o_self[1])
    w_up = plane_gather(net, up_line).reshape(width, hidden // 2)
    mem_page = line_gather(net, mem, 0).reshape(-1, width)
    down_line = line_gather_held(net, after(ff_out, o_self[1]), 0, attended)
    w_down = plane_gather(net, down_line).reshape(hidden // 2, width)
    mem_all = jnp.concatenate([mem_page, net.sibling(mem_page)], axis=0)
    mem_rows = mem_page.shape[0]
    b_kv = jnp.concatenate([jnp.zeros((half,), F32), halves(bias[4])])
    kv_cross = (dot(mem_all, w_cross_kv) + b_kv).astype(BF16)
    kv_own, kv_other = kv_cross[:mem_rows], kv_cross[mem_rows:]


    def summed(rows_two, weight, dims=NN):
        sent = dot(rows_two[rows:], weight, dims).astype(BF16)
        back = net.sibling(sent)
        return dot(rows_two[:rows], weight, dims) + back.astype(F32)

    def both_pages(value):
        return jnp.concatenate([value, net.sibling(value)], axis=0)

    w_self_out = turned(w_self_out, z)
    x_in = tok.astype(F32)
    x_one = x_in + summed(attended, w_self_out) + bias[2]

    h_two = both_pages(layer_norm(x_one, gain[1], shift[1]))
    q_cross = (dot(h_two, w_cross_q) + halves(bias[3])).astype(BF16)
    oc_own, lse_own = cross_fwd(limit_own, q_cross[:rows], kv_own)
    oc_other, lse_other = cross_fwd(limit_other, q_cross[rows:], kv_other)
    o_cross = jnp.concatenate([oc_own, oc_other], axis=0)
    x_two = x_one + summed(o_cross, w_cross_out) + bias[5]

    h_three = both_pages(layer_norm(x_two, gain[2], shift[2]))
    pre_act = dot(h_three, w_up) + up_bias
    cdf = 0.5 + 0.5 * lax.erf(pre_act * (0.5**0.5))
    act = (pre_act * cdf).astype(BF16)
    layer_rows = (x_two + summed(act, w_down) + bias[6]).astype(BF16)

    slope = cdf + pre_act * (jnp.exp(-0.5 * pre_act * pre_act) * 0.3989422804014327)
    g_pre = (dot(cot_two, w_down, NT) * slope).astype(BF16)
    grad_down = dot(act, cot_two, TN).astype(BF16)
    grad_up = dot(h_three, g_pre, TN).astype(BF16)
    part_down = plane_scatter(net, grad_down.reshape(chips, seq, ff_shard, width))
    part_up = plane_scatter(net, grad_up.reshape(chips, 2, seq, shard, hidden // 2))
    cot_wide = cot.astype(F32)
    back, d_gain2, d_shift2 = norm_back(x_two, gain[2], summed(g_pre, w_up, NT))
    g_two = cot_wide + back

    g_cross = both_pages(after(g_two.astype(BF16), grad_down, grad_up))
    grad_cross_out = dot(o_cross, g_cross, TN).astype(BF16)
    d_oc = dot(g_cross, w_cross_out, NT).astype(BF16)
    sum_down = line_scatter(net, after(part_down, g_cross), 0)
    dq_own, dk_own, dv_own = cross_bwd(
        limit_own, q_cross[:rows], kv_own, d_oc[:rows], oc_own, lse_own
    )
    dq_other, dk_other, dv_other = cross_bwd(
        limit_other, q_cross[rows:], kv_other, d_oc[rows:], oc_other, lse_other
    )
    dq_cross = jnp.concatenate([dq_own, dq_other], axis=0)
    dq_cross = after(dq_cross, sum_down)
    dkv_own = jnp.concatenate([dk_own, dv_own], axis=1)
    dkv_other = jnp.concatenate([dk_other, dv_other], axis=1)
    dkv_cross = jnp.concatenate([dkv_own, dkv_other], axis=0)
    grad_cross = jnp.concatenate(
        [dot(h_two, dq_cross, TN).astype(BF16), dot(mem_all, dkv_cross, TN).astype(BF16)], axis=1
    )
    part_cross = plane_scatter(net, grad_cross.reshape(chips, 2, seq, shard, 3 * half))
    mem_sent = dot(dkv_other, w_cross_kv, NT).astype(BF16)
    mem_grad = dot(dkv_own, w_cross_kv, NT) + net.sibling(mem_sent).astype(F32)
    back, d_gain1, d_shift1 = norm_back(x_one, gain[1], summed(dq_cross, w_cross_q, NT))
    g_one = g_two + back

    g_self = both_pages(after(g_one.astype(BF16), grad_cross))
    grad_self_out = turned(dot(attended, g_self, TN).astype(BF16), lax.rem(seq - z, seq))
    grad_outs = jnp.concatenate([grad_self_out, grad_cross_out], axis=1)
    part_outs = plane_scatter(net, grad_outs.reshape(chips, seq, shard, 2 * width))
    d_os = to_heads(dot(g_self, w_self_out, NT).astype(BF16))
    sum_up = jnp.concatenate([part_up[0], part_up[1]], axis=1)
    sum_up = seq_scatter(sum_up).reshape(2, shard, hidden // 2)
    d_os = after(d_os, grad_outs, sum_up)
    grad_memory = seq_scatter(after(mem_grad, part_outs).reshape(seq, -1, width).astype(BF16))
    page_grads, d_hs = [], []
    for k in range(2):
        lse = after(lse_self[k], here, part_cross) if k else lse_self[k]
        page_grad = self_bwd(qkv, d_os, o_self[k], lse, att_rows, k)[0]
        page_grads.append(page_grad)
        sides = w_qkv.reshape(2, half, 3 * lanes)
        there = dot(page_grad, pick(sides, 1 - core), NT).astype(BF16)
        here = dot(page_grad, pick(sides, core), NT) + net.sibling(there).astype(F32)
        d_hs.append(line_two_way_scatter(net, here.reshape(seq, rows, half)))
    own, other = own_first(net, jnp.stack(d_hs))
    other = net.sibling(other)
    d_h = jnp.concatenate(
        [jnp.where(core == 0, own, other), jnp.where(core == 0, other, own)], axis=1
    )
    last = seq_scatter(jnp.concatenate([part_cross[0], part_cross[1], part_outs], axis=2))
    sum_outs = last[:, 6 * half :]
    sum_cross = jnp.stack([last[:, : 3 * half], last[:, 3 * half : 6 * half]])
    columns = jnp.concatenate([sum_up, sum_cross], axis=2)
    own, other = own_first(net, columns)
    other = net.sibling(other)
    sides = [jnp.where(core == k, own, other) for k in range(2)]

    def joined(at, count):
        two = jnp.stack([side[:, at : at + count] for side in sides], axis=1)
        return join_halves(two)

    sum_up = joined(0, hidden // 2)
    sum_cross = jnp.stack([joined(hidden // 2 + k * half, half) for k in range(3)])
    flat = after(jnp.concatenate(page_grads, axis=0), here, part_outs)
    back, _, _ = norm_back(x_in, gain[0], d_h)
    token_grad = g_one + back

    def spread(vector):
        split = vector.reshape(pages // 2, 1, width // pages)
        here = jnp.arange(2)[None, :, None] == core
        return jnp.where(here, split, 0.0).reshape(width)

    def spread_heads(vector):
        return lax.dynamic_update_slice_in_dim(jnp.zeros((width,), F32), vector, first, 0)

    sums_qkv = column_sum(flat)
    grad_qkv = dot(h_all, flat, TN)
    w_wide = w_qkv.astype(F32)
    by_row = (grad_qkv - shift[0][:, None] * sums_qkv) / gain[0][:, None]
    d_gain0 = jnp.sum(w_wide * by_row, axis=1)
    d_shift0 = jnp.sum(w_wide * sums_qkv, axis=1)
    up_sum = column_sum(g_pre).reshape(chips, 1, seq * ff_shard)
    up_sum = jnp.where(jnp.arange(2)[None, :, None] == core, up_sum, 0.0)
    vectors = jnp.stack(
        [
            d_gain0,
            d_gain1,
            d_gain2,
            d_shift0,
            d_shift1,
            d_shift2,
            spread_heads(sums_qkv[:lanes]),
            spread_heads(sums_qkv[2 * lanes :]),
            column_sum(g_one),
            spread(column_sum(dq_cross)),
            spread(column_sum(dkv_cross[:, half:])),
            column_sum(g_two),
            column_sum(cot_wide),
        ]
    )
    small = jnp.concatenate([vectors.T, up_sum.reshape(width, ff_shard // shard)], axis=1)
    small = jnp.pad(small, ((0, 0), (0, side - small.shape[1])))
    parts = jnp.concatenate([grad_qkv.astype(BF16), small.astype(BF16)], axis=1)
    parts = ring_scatter(net, parts.reshape(chips, 2, seq * shard, 3 * lanes + side))
    parts = parts.reshape(2, seq, shard, 3 * lanes + side)
    low = parts.astype(BF16)
    piece = jnp.zeros((2, seq, shard, 3 * lanes), BF16)
    piece = put(piece, pick(low, z, 1)[..., : 3 * lanes], z, 1)
    small = pick(parts, z, 1)[..., 3 * lanes :]
    for s in range(1, seq):
        got = net.along(pick(low, net.z_at(s), 1), s)
        piece = put(piece, got[..., : 3 * lanes], net.z_at(-s), 1)
        small += got[..., 3 * lanes :].astype(F32)
    own, other = own_first(net, piece)
    piece = by_core(net, own, net.sibling(other))
    sum_self = piece.reshape(2, seq, shard, 3, lanes).transpose(3, 2, 1, 0, 4)
    sum_self = sum_self.reshape(3, shard, width).astype(F32)
    own, other = own_first(net, small)
    small = own + net.sibling(other)
    vectors = small[:, :13].T
    return (
        layer_rows[None],
        token_grad[None],
        grad_memory[None],
        vectors[0:3],
        vectors[3:6],
        sum_self,
        sum_outs[:, :width],
        sum_cross,
        sum_outs[:, width:],
        sum_up,
        sum_down,
        vectors[6:13],
        small[:, 13 : 13 + ff_shard // shard].reshape(ff_shard),
    )


def solution(mesh):
    weight = P(AXES, None)
    return jax.shard_map(
        functools.partial(on_device, mesh=mesh),
        mesh=mesh,
        in_specs=(
            P("page", "seq", None),
            P("page", "seq", None),
            P("page", "seq", None),
            P("page"),
            P(None, AXES),
            P(None, AXES),
            P(None, AXES, None),
            weight,
            P(None, AXES, None),
            weight,
            weight,
            weight,
            P(None, AXES),
            P(AXES),
        ),
        out_specs=(
            P("page", "seq", None),
            P("page", "seq", None),
            P("page", "seq", None),
            P(None, AXES),
            P(None, AXES),
            P(None, AXES, None),
            weight,
            P(None, AXES, None),
            weight,
            weight,
            weight,
            P(None, AXES),
            P(AXES),
        ),
        check_vma=False,
    )
```

```python
import functools

import jax
import jax.numpy as jnp
from jax import lax
from jax.experimental import pallas as pl
from jax.experimental.pallas import tpu as pltpu
from jax.sharding import PartitionSpec as P

HEADS = 16
HEAD_DIM = 64
VALID_HI = 588
VALID_LO = 140

NEGATIVE = -1e30
EPSILON = 1e-05
LOG2E = 1.4426950408889634
SCALING = HEAD_DIM ** (-0.5)
AXES = ("page", "seq")
F32 = jnp.float32
BF16 = jnp.bfloat16
NT = (((1,), (1,)), ((), ()))
NN = (((1,), (0,)), ((), ()))
TN = (((0,), (0,)), ((), ()))


def dot(a, b, dims=NN):
    return lax.dot_general(a, b, dims, preferred_element_type=F32)


def project_kernel(spot_ref, x_ref, gain_ref, shift_ref, w_ref, b_ref, h_in, qkv_in, h_ref, qkv_ref):
    del spot_ref, h_in, qkv_in
    x = x_ref[...].astype(F32)
    centered = x - jnp.mean(x, axis=-1, keepdims=True)
    scale = lax.rsqrt(jnp.mean(centered * centered, axis=-1, keepdims=True) + EPSILON)
    h = (centered * scale * gain_ref[...] + shift_ref[...]).astype(BF16)
    h_ref[0, 0] = h
    qkv_ref[0, 0] = (dot(h, w_ref[...]) + b_ref[...]).astype(BF16)


def project(spot, x, gain, shift, w_qkv, b_qkv, h_all, qkv):
    rows, width = x.shape
    wide = w_qkv.shape[1]
    block = min(256, rows)
    whole = lambda shape: pl.BlockSpec(shape, lambda i, n: (0, 0))
    return pl.pallas_call(
        project_kernel,
        grid_spec=pltpu.PrefetchScalarGridSpec(
            num_scalar_prefetch=1,
            grid=(rows // block,),
            in_specs=[
                pl.BlockSpec((block, width), lambda i, n: (i, 0)),
                whole((1, width)),
                whole((1, width)),
                whole((width, wide)),
                whole((1, wide)),
                pl.BlockSpec(memory_space=pl.ANY),
                pl.BlockSpec(memory_space=pl.ANY),
            ],
            out_specs=[
                pl.BlockSpec((1, 1, block, width), lambda i, n: (n[0], n[1], i, 0)),
                pl.BlockSpec((1, 1, block, wide), lambda i, n: (n[0], n[1], i, 0)),
            ],
        ),
        out_shape=[
            jax.ShapeDtypeStruct(h_all.shape, BF16),
            jax.ShapeDtypeStruct(qkv.shape, BF16),
        ],
        input_output_aliases={6: 0, 7: 1},
        compiler_params=pltpu.CompilerParams(vmem_limit_bytes=32 * 1024 * 1024),
        cost_estimate=pl.CostEstimate(
            flops=2 * rows * width * wide, bytes_accessed=4 * rows * width, transcendentals=0
        ),
    )(spot, x, gain[None], shift[None], w_qkv, b_qkv[None], h_all, qkv)


def self_fwd_kernel(order_ref, q_ref, kv_ref, o_ref, lse_ref, *, rows, width):
    del order_ref
    i = pl.program_id(1)
    heads = width // HEAD_DIM
    queries = [q_ref[0, :, h * HEAD_DIM : (h + 1) * HEAD_DIM] for h in range(heads)]
    ones = jnp.ones((16, rows), BF16)

    def step(j, carry, diagonal):
        at = pl.ds(pl.multiple_of(j * rows, rows), rows)
        keys_all = kv_ref[0, at, width : 2 * width]
        values_t = kv_ref[0, at, 2 * width : 3 * width].T
        out = []
        for h in range(heads):
            run_max, acc = carry[h]
            lanes = slice(h * HEAD_DIM, (h + 1) * HEAD_DIM)
            scores = dot(keys_all[:, lanes], queries[h], NT) * (SCALING * LOG2E)
            if diagonal:
                place_k = lax.broadcasted_iota(jnp.int32, (rows, rows), 0)
                place_q = lax.broadcasted_iota(jnp.int32, (rows, rows), 1)
                scores = jnp.where(place_k <= place_q, scores, NEGATIVE)
            new_max = jnp.maximum(run_max, jnp.max(scores, axis=0, keepdims=True))
            probs = jnp.exp2(scores - new_max).astype(BF16)
            wide = jnp.concatenate([values_t[lanes], ones], axis=0)
            out.append((new_max, acc * jnp.exp2(run_max - new_max) + dot(wide, probs)))
        return tuple(out)

    start = tuple(
        (jnp.full((1, rows), NEGATIVE, F32), jnp.zeros((HEAD_DIM + 16, rows), F32))
        for _ in range(heads)
    )
    carry = lax.fori_loop(0, i, lambda j, c: step(j, c, False), start)
    carry = step(i, carry, True)
    outs = []
    for h in range(heads):
        run_max, acc = carry[h]
        total = acc[HEAD_DIM : HEAD_DIM + 1]
        outs.append(acc[:HEAD_DIM] / total)
        lse_ref[0, h] = run_max + jnp.log2(total)
    o_ref[0] = jnp.concatenate(outs, axis=0).T.astype(BF16)


def self_fwd(order, qkv, rows, page):
    length, three = qkv.shape[1:]
    width = three // 3
    heads = width // HEAD_DIM
    cost = heads * length * length * HEAD_DIM * 2
    return pl.pallas_call(
        functools.partial(self_fwd_kernel, rows=rows, width=width),
        grid=(1, length // rows),
        in_specs=[
            pl.BlockSpec(memory_space=pltpu.SMEM),
            pl.BlockSpec((1, rows, three), lambda p, i: (page, i, 0)),
            pl.BlockSpec((1, length, three), lambda p, i: (page, 0, 0)),
        ],
        out_specs=[
            pl.BlockSpec((1, rows, width), lambda p, i: (0, i, 0)),
            pl.BlockSpec((1, heads, 1, rows), lambda p, i: (0, 0, 0, i)),
        ],
        out_shape=[
            jax.ShapeDtypeStruct((1, length, width), BF16),
            jax.ShapeDtypeStruct((1, heads, 1, length), F32),
        ],
        compiler_params=pltpu.CompilerParams(vmem_limit_bytes=48 * 1024 * 1024),
        cost_estimate=pl.CostEstimate(
            flops=2 * cost, bytes_accessed=4 * qkv.size, transcendentals=cost // 256
        ),
    )(order, qkv, qkv)


def self_bwd_kernel(q_ref, kv_ref, do_ref, o_ref, lse_ref, out_ref, dk_acc, dv_acc, *, rows, width):
    i = pl.program_id(1)
    heads = width // HEAD_DIM

    @pl.when(i == 0)
    def _():
        dk_acc[...] = jnp.zeros_like(dk_acc)
        dv_acc[...] = jnp.zeros_like(dv_acc)

    q_all = q_ref[0, :, :width]
    do_all = do_ref[0]
    prod = (do_all.astype(F32) * o_ref[0].astype(F32)).T
    per_head = [slice(h * HEAD_DIM, (h + 1) * HEAD_DIM) for h in range(heads)]
    deltas = [jnp.sum(prod[s], axis=0, keepdims=True) for s in per_head]

    def step(j, carry, diagonal):
        at = pl.ds(pl.multiple_of(j * rows, rows), rows)
        k_all = kv_ref[0, at, width : 2 * width]
        v_all = kv_ref[0, at, 2 * width : 3 * width]
        k_t = k_all.T
        new, dks, dvs = [], [], []
        for h in range(heads):
            s = per_head[h]
            scores = dot(k_all[:, s], q_all[:, s], NT) * (SCALING * LOG2E)
            probs = jnp.exp2(scores - lse_ref[0, h])
            if diagonal:
                place_k = lax.broadcasted_iota(jnp.int32, (rows, rows), 0)
                place_q = lax.broadcasted_iota(jnp.int32, (rows, rows), 1)
                probs = jnp.where(place_k <= place_q, probs, 0.0)
            d_probs = dot(v_all[:, s], do_all[:, s], NT)
            d_scores = (probs * (d_probs - deltas[h])).astype(BF16)
            dvs.append(dot(probs.astype(BF16), do_all[:, s]))
            dks.append(dot(d_scores, q_all[:, s]))
            new.append(carry[h] + dot(k_t[s], d_scores))
        dk_acc[at, :] += jnp.concatenate(dks, axis=1)
        dv_acc[at, :] += jnp.concatenate(dvs, axis=1)
        return tuple(new)

    start = tuple(jnp.zeros((HEAD_DIM, rows), F32) for _ in range(heads))
    carry = lax.fori_loop(0, i, lambda j, c: step(j, c, False), start)
    carry = step(i, carry, True)
    dq = (jnp.concatenate(carry, axis=0) * SCALING).T.astype(BF16)
    out_ref[0, pl.ds(pl.multiple_of(i * rows, rows), rows), :width] = dq

    @pl.when(i == pl.num_programs(1) - 1)
    def _():
        out_ref[0, :, width : 2 * width] = (dk_acc[...] * SCALING).astype(BF16)
        out_ref[0, :, 2 * width :] = dv_acc[...].astype(BF16)


def self_bwd(qkv, d_out, out, lse, rows, page):
    length, three = qkv.shape[1:]
    width = three // 3
    heads = width // HEAD_DIM
    cost = heads * length * length * HEAD_DIM * 5
    return pl.pallas_call(
        functools.partial(self_bwd_kernel, rows=rows, width=width),
        grid=(1, length // rows),
        in_specs=[
            pl.BlockSpec((1, rows, three), lambda p, i: (page, i, 0)),
            pl.BlockSpec((1, length, three), lambda p, i: (page, 0, 0)),
            pl.BlockSpec((1, rows, width), lambda p, i: (page, i, 0)),
            pl.BlockSpec((1, rows, width), lambda p, i: (0, i, 0)),
            pl.BlockSpec((1, heads, 1, rows), lambda p, i: (0, 0, 0, i)),
        ],
        out_specs=pl.BlockSpec((1, length, three), lambda p, i: (0, 0, 0)),
        out_shape=jax.ShapeDtypeStruct((1, length, three), BF16),
        scratch_shapes=[pltpu.VMEM((length, width), F32), pltpu.VMEM((length, width), F32)],
        compiler_params=pltpu.CompilerParams(vmem_limit_bytes=48 * 1024 * 1024),
        cost_estimate=pl.CostEstimate(
            flops=2 * cost, bytes_accessed=6 * qkv.size, transcendentals=cost // 640
        ),
    )(qkv, qkv, d_out, out, lse)


def cross_fwd_kernel(limit_ref, q_ref, k_ref, v_ref, o_ref, lse_ref):
    limit = limit_ref[0]
    rows, mem = q_ref.shape[0], k_ref.shape[0]
    valid = lax.broadcasted_iota(jnp.int32, (mem, rows), 0) < limit
    values_t = v_ref[...].T
    ones = jnp.ones((16, mem), BF16)
    outs = []
    for h in range(2):
        s = slice(h * HEAD_DIM, (h + 1) * HEAD_DIM)
        scores = dot(k_ref[:, s], q_ref[:, s], NT) * (SCALING * LOG2E)
        scores = jnp.where(valid, scores, NEGATIVE)
        top = jnp.max(scores, axis=0, keepdims=True)
        probs = jnp.exp2(scores - top).astype(BF16)
        acc = dot(jnp.concatenate([values_t[s], ones], axis=0), probs)
        total = acc[HEAD_DIM : HEAD_DIM + 1]
        outs.append(acc[:HEAD_DIM] / total)
        lse_ref[0, h : h + 1] = top + jnp.log2(total)
    o_ref[...] = jnp.concatenate(outs, axis=0).T.astype(BF16)


def cross_fwd(limit, q, kv):
    rows, width = q.shape
    mem = kv.shape[0]
    pairs = width // (2 * HEAD_DIM)
    wide = 2 * HEAD_DIM
    cost = width * rows * mem * 2
    return pl.pallas_call(
        cross_fwd_kernel,
        grid_spec=pltpu.PrefetchScalarGridSpec(
            num_scalar_prefetch=1,
            grid=(pairs,),
            in_specs=[
                pl.BlockSpec((rows, wide), lambda p, n: (0, p)),
                pl.BlockSpec((mem, wide), lambda p, n: (0, p)),
                pl.BlockSpec((mem, wide), lambda p, n: (0, p + pairs)),
            ],
            out_specs=[
                pl.BlockSpec((rows, wide), lambda p, n: (0, p)),
                pl.BlockSpec((1, 2, rows), lambda p, n: (p, 0, 0)),
            ],
        ),
        out_shape=[
            jax.ShapeDtypeStruct((rows, width), BF16),
            jax.ShapeDtypeStruct((pairs, 2, rows), F32),
        ],
        compiler_params=pltpu.CompilerParams(vmem_limit_bytes=48 * 1024 * 1024),
        cost_estimate=pl.CostEstimate(
            flops=2 * cost, bytes_accessed=4 * (q.size + kv.size), transcendentals=cost // 128
        ),
    )(limit, q, kv, kv)


def cross_bwd_kernel(limit_ref, q_ref, k_ref, v_ref, do_ref, o_ref, lse_ref, dq_ref, dk_ref, dv_ref):
    limit = limit_ref[0]
    rows, mem = q_ref.shape[0], k_ref.shape[0]
    valid = lax.broadcasted_iota(jnp.int32, (mem, rows), 0) < limit
    k_t = k_ref[...].T
    prod = (do_ref[...].astype(F32) * o_ref[...].astype(F32)).T
    dqs, dks, dvs = [], [], []
    for h in range(2):
        s = slice(h * HEAD_DIM, (h + 1) * HEAD_DIM)
        delta = jnp.sum(prod[s], axis=0, keepdims=True)
        scores = dot(k_ref[:, s], q_ref[:, s], NT) * (SCALING * LOG2E)
        scores = jnp.where(valid, scores, NEGATIVE)
        probs = jnp.exp2(scores - lse_ref[0, h : h + 1])
        d_probs = dot(v_ref[:, s], do_ref[:, s], NT)
        d_scores = (probs * (d_probs - delta)).astype(BF16)
        dvs.append(dot(probs.astype(BF16), do_ref[:, s]))
        dks.append(dot(d_scores, q_ref[:, s]))
        dqs.append(dot(k_t[s], d_scores))
    dq_ref[...] = (jnp.concatenate(dqs, axis=0) * SCALING).T.astype(BF16)
    dk_ref[...] = (jnp.concatenate(dks, axis=1) * SCALING).astype(BF16)
    dv_ref[...] = jnp.concatenate(dvs, axis=1).astype(BF16)


def cross_bwd(limit, q, kv, d_out, out, lse):
    rows, width = q.shape
    mem = kv.shape[0]
    pairs = width // (2 * HEAD_DIM)
    wide = 2 * HEAD_DIM
    cost = width * rows * mem * 5
    token_block = pl.BlockSpec((rows, wide), lambda p, n: (0, p))
    memory_block = pl.BlockSpec((mem, wide), lambda p, n: (0, p))
    return pl.pallas_call(
        cross_bwd_kernel,
        grid_spec=pltpu.PrefetchScalarGridSpec(
            num_scalar_prefetch=1,
            grid=(pairs,),
            in_specs=[
                token_block,
                memory_block,
                pl.BlockSpec((mem, wide), lambda p, n: (0, p + pairs)),
                token_block,
                token_block,
                pl.BlockSpec((1, 2, rows), lambda p, n: (p, 0, 0)),
            ],
            out_specs=[token_block, memory_block, memory_block],
        ),
        out_shape=[
            jax.ShapeDtypeStruct((rows, width), BF16),
            jax.ShapeDtypeStruct((mem, width), BF16),
            jax.ShapeDtypeStruct((mem, width), BF16),
        ],
        compiler_params=pltpu.CompilerParams(vmem_limit_bytes=48 * 1024 * 1024),
        cost_estimate=pl.CostEstimate(
            flops=2 * cost, bytes_accessed=6 * (q.size + kv.size), transcendentals=cost // 320
        ),
    )(limit, q, kv, kv, d_out, out, lse)


def gray(n):
    return n ^ (n >> 1)


class Net:
    def __init__(self, mesh):
        self.pages, self.seq = mesh.shape["page"], mesh.shape["seq"]
        self.chips = self.pages // 2
        page = lax.axis_index("page")
        self.core = lax.rem(page, 2)
        self.chip = lax.div(page, 2)
        self.z = lax.axis_index("seq")
        place = self.chip
        shift = 1
        while (self.chips - 1) >> shift:
            place = place ^ (self.chip >> shift)
            shift += 1
        self.place = place
        where = {gray(j): j for j in range(self.chips)}

        def index(chip, core, z):
            return (chip * 2 + core) * self.seq + z

        everyone = [
            (chip, core, z)
            for chip in range(self.chips)
            for core in range(2)
            for z in range(self.seq)
        ]
        self.planes = [
            [index(chip, core, z) for chip in range(self.chips)]
            for core in range(2)
            for z in range(self.seq)
        ]
        self.pair_map = [(index(h, c, z), index(h, 1 - c, z)) for h, c, z in everyone]
        self.line_map = [
            [(index(h, c, z), index(h, c, (z + s) % self.seq)) for h, c, z in everyone]
            for s in range(self.seq)
        ]
        self.ring_map = {
            way: [
                (index(h, c, z), index(gray((where[h] + way) % self.chips), c, z))
                for h, c, z in everyone
            ]
            for way in (1, -1)
        }

    def sibling(self, value):
        return lax.ppermute(value, AXES, self.pair_map)

    def along(self, value, by):
        return lax.ppermute(value, AXES, self.line_map[by % self.seq])

    def around(self, value, way):
        return lax.ppermute(value, AXES, self.ring_map[way])

    def chip_at(self, by):
        j = lax.rem(self.place + by + self.chips, self.chips)
        return j ^ (j >> 1)

    def z_at(self, by):
        return lax.rem(self.z + by + self.seq, self.seq)


def put(buffer, piece, index, axis):
    return lax.dynamic_update_slice_in_dim(buffer, jnp.expand_dims(piece, axis), index, axis)


def pick(buffer, index, axis=0):
    return lax.dynamic_index_in_dim(buffer, index, axis, keepdims=False)


def line_pieces(net, piece):
    yield 0, piece
    right, left = piece, piece
    for t in range(1, net.seq // 2 + 1):
        right = net.along(right, 1)
        yield -t, right
        if t <= (net.seq - 1) // 2:
            left = net.along(left, -1)
            yield t, left


def line_gather(net, piece, axis):
    out = jnp.zeros(piece.shape[:axis] + (net.seq,) + piece.shape[axis:], piece.dtype)
    for by, got in line_pieces(net, piece):
        out = put(out, got, net.z_at(by), axis)
    return out


def line_gather_held(net, piece, axis, *others):
    out = put(jnp.zeros(piece.shape[:axis] + (net.seq,) + piece.shape[axis:], piece.dtype), piece, net.z, axis)
    for s in range(1, net.seq):
        out = put(out, after(net.along(piece, s), *others), net.z_at(-s), axis)
    return out


def ring_gather(net, piece):
    half = piece.shape[0] // 2
    out = put(jnp.zeros((net.chips,) + piece.shape, piece.dtype), piece, net.chip, 0)
    right, left = piece, piece
    for t in range(1, net.chips // 2):
        right, left = net.around(right, 1), net.around(left, -1)
        out = put(out, right, net.chip_at(-t), 0)
        out = put(out, left, net.chip_at(t), 0)
    far = net.chip_at(net.chips // 2)
    right, left = net.around(right[:half], 1), net.around(left[half:], -1)
    return put(out, jnp.concatenate([right, left], axis=0), far, 0)


def ring_scatter(net, parts):
    half = parts.shape[1] // 2
    steps = net.chips // 2
    far = pick(parts, net.chip_at(steps))
    right, left = net.around(far[:half], 1), net.around(far[half:], -1)
    for t in range(1, steps):
        k = steps - t
        mine = pick(parts, net.chip_at(k))
        if t == 1:
            first = mine[:half].astype(F32) + right.astype(F32)
            sent = jnp.concatenate([first.astype(BF16), mine[half:]], axis=0)
        else:
            sent = (mine.astype(F32) + right.astype(F32)).astype(BF16)
        mine = pick(parts, net.chip_at(-k))
        if t == 1:
            first = mine[half:].astype(F32) + left.astype(F32)
            back = jnp.concatenate([mine[:half], first.astype(BF16)], axis=0)
        else:
            back = (mine.astype(F32) + left.astype(F32)).astype(BF16)
        right, left = net.around(sent, 1), net.around(back, -1)
    return pick(parts, net.chip).astype(F32) + right.astype(F32) + left.astype(F32)


def line_scatter(net, parts, axis):
    low = parts.astype(BF16)
    sent = [pick(low, net.z_at(s), axis) for s in range(1, net.seq)]
    got = [net.along(value, s + 1) for s, value in enumerate(sent)]
    return pick(parts, net.z, axis).astype(F32) + sum(value.astype(F32) for value in got)


def own_first(net, value):
    return pick(value, net.core), pick(value, 1 - net.core)


def by_core(net, own, other):
    return jnp.where(net.core == 0, jnp.stack([own, other]), jnp.stack([other, own]))


def plane_gather(net, piece):
    return lax.all_gather(piece, AXES, axis=0, axis_index_groups=net.planes)


def plane_scatter(net, parts):
    flat = parts.reshape(-1, parts.shape[-1])
    mine = lax.psum_scatter(
        flat, AXES, scatter_dimension=0, axis_index_groups=net.planes, tiled=True
    )
    return mine.reshape(parts.shape[1:])


def seq_scatter(parts):
    flat = parts.reshape(-1, parts.shape[-1])
    mine = lax.psum_scatter(flat, "seq", scatter_dimension=0, tiled=True)
    return mine.reshape(parts.shape[1:]).astype(F32)


def after(value, *others):
    for other in others:
        element = lax.optimization_barrier(other)[(0,) * other.ndim].astype(F32)
        value = value + jnp.minimum(jnp.abs(element), 0.0).astype(value.dtype)
    return value


def scatter_columns(net, grad, rows):
    parts = grad.reshape(net.chips, 2, net.seq, rows, grad.shape[-1])
    mine = line_scatter(net, plane_scatter(net, parts), 1)
    own, other = own_first(net, mine)
    return jnp.moveaxis(by_core(net, own, net.sibling(other)), 0, 1)


def scatter_rows(net, grad, rows):
    parts = grad.reshape(net.chips, net.seq, rows, grad.shape[-1])
    return line_scatter(net, plane_scatter(net, parts), 0)


def line_two_way_scatter(net, parts, hold=()):
    total = pick(parts, net.z)
    for way, far in ((1, net.seq // 2), (-1, (net.seq - 1) // 2)):
        got = None
        for by in range(far, 0, -1):
            mine = pick(parts, net.z_at(way * by))
            sent = mine.astype(BF16) if got is None else after((mine + got).astype(BF16), *hold)
            got = net.along(sent, way).astype(F32)
        if got is not None:
            total += got
    return total


def norm_parts(values):
    centered = values - jnp.mean(values, axis=-1, keepdims=True)
    scale = lax.rsqrt(jnp.mean(centered * centered, axis=-1, keepdims=True) + EPSILON)
    return centered * scale, scale


def layer_norm(values, gain, shift):
    return (norm_parts(values)[0] * gain + shift).astype(BF16)


def norm_back(values, gain, upstream):
    normed, scale = norm_parts(values)
    scaled = upstream * gain
    mean_g = jnp.mean(scaled, axis=-1, keepdims=True)
    mean_gn = jnp.mean(scaled * normed, axis=-1, keepdims=True)
    grad = (scaled - mean_g - normed * mean_gn) * scale
    return grad, jnp.sum(upstream * normed, axis=0), jnp.sum(upstream, axis=0)


def column_sum(values):
    return jnp.sum(values.astype(F32), axis=0)


def on_device(
    tokens,
    memory,
    cotangent,
    res_flag,
    ln_gain,
    ln_bias,
    self_in,
    self_out,
    cross_in,
    cross_out,
    ff_in,
    ff_out,
    proj_bias,
    ff_bias,
    *,
    mesh,
):
    net = Net(mesh)
    core, z = net.core, net.z
    rows, width = tokens.shape[1], tokens.shape[2]
    seq, chips, pages = net.seq, net.chips, net.pages
    shard = self_in.shape[1]
    hidden = ff_in.shape[1]
    ff_shard = ff_out.shape[0]
    lanes = width // (2 * seq)
    half = width // 2
    tok, mem, cot = tokens[0], memory[0], cotangent[0]

    def halves(vector):
        return pick(vector.reshape(pages // 2, 2, width // pages), core, 1).reshape(half)

    def column_halves(weight):
        lead, columns = weight.shape[:-1], weight.shape[-1]
        split = weight.reshape(lead + (pages // 2, 2, columns // pages))
        return jnp.moveaxis(split, -2, -3).reshape(lead + (2, columns // 2))

    def join_halves(weight):
        lead, columns = weight.shape[:-2], weight.shape[-1] * 2
        split = weight.reshape(lead + (2, pages // 2, columns // pages))
        return jnp.moveaxis(split, -3, -2).reshape(lead + (columns,))

    side = 128
    small = jnp.concatenate(
        [
            ln_gain.T,
            ln_bias.T,
            proj_bias.T,
            jnp.broadcast_to(res_flag.astype(BF16)[:, None], (shard, 1)),
            ff_bias.reshape(shard, ff_shard // shard),
        ],
        axis=1,
    )
    small = jnp.pad(small, ((0, 0), (0, side - small.shape[1])))
    blocks = self_in.reshape(3, shard, seq, 2, lanes).transpose(3, 2, 1, 0, 4)
    blocks = blocks.reshape(2, seq, shard, 3 * lanes)
    small = jnp.broadcast_to(small, (2, seq, shard, side))
    blocks = jnp.concatenate([blocks, small], axis=3)
    own, other = own_first(net, blocks)
    blocks = by_core(net, own, net.sibling(other))
    piece = jnp.zeros_like(blocks)
    piece = put(piece, pick(blocks, z, 1), z, 1)
    for s in range(1, seq):
        piece = put(piece, net.along(pick(blocks, net.z_at(s), 1), s), net.z_at(-s), 1)
    qkv_line = piece
    w_wide = ring_gather(net, piece).reshape(width, 3 * lanes + side)
    w_qkv = w_wide[:, : 3 * lanes]
    small = w_wide[:, 3 * lanes :].astype(F32)
    vectors = small[:, :13].T
    gain, shift, bias = vectors[0:3], vectors[3:6], vectors[6:13]
    flags = small[:, 13].reshape(pages, seq * shard)[:, 0]
    up_bias = small[:, 14 : 14 + ff_shard // shard].reshape(chips, 2, seq * ff_shard)
    up_bias = pick(up_bias, core, 1).reshape(hidden // 2)
    page = lax.axis_index("page")

    def limit_of(which):
        return jnp.where(pick(flags, which) > 0.5, VALID_HI, VALID_LO).astype(jnp.int32).reshape(1)

    limit_own, limit_other = limit_of(page), limit_of(page ^ 1)

    limit_own, limit_other = limit_of(page), limit_of(page ^ 1)
    first = (2 * z + core) * lanes
    b_qkv = jnp.concatenate(
        [
            lax.dynamic_slice_in_dim(bias[0], first, lanes),
            jnp.zeros((lanes,), F32),
            lax.dynamic_slice_in_dim(bias[1], first, lanes),
        ]
    )

    cross_halves = column_halves(cross_in).transpose(2, 1, 0, 3).reshape(2, shard, 3 * half)
    column_parts = jnp.concatenate([cross_halves, column_halves(ff_in).transpose(1, 0, 2)], axis=2)
    own, other = own_first(net, column_parts)
    column_parts = by_core(net, own, net.sibling(other))
    cross_parts, up_parts = column_parts[:, :, : 3 * half], column_parts[:, :, 3 * half :]
    bundle = jnp.concatenate([cross_parts[0], cross_parts[1], self_out, cross_out], axis=1)
    bundle_line = line_gather(net, after(bundle, qkv_line), 0)
    bundle = plane_gather(net, bundle_line)

    def rows_of(at, columns):
        two = [bundle[..., c * 3 * half + at : c * 3 * half + at + columns] for c in range(2)]
        return jnp.stack(two, axis=1).reshape(width, columns)

    w_cross_q, w_cross_kv = rows_of(0, half), rows_of(half, width)
    w_self_out = bundle[..., 6 * half : 6 * half + width].reshape(half, width)
    w_cross_out = bundle[..., 6 * half + width :].reshape(half, width)
    h_all = jnp.zeros((2, seq, rows, width), BF16)
    qkv = jnp.zeros((2, seq, rows, 3 * lanes), BF16)
    right = left = passing = after(tok, qkv_line)
    for t in range(seq // 2 + 1):
        if t == 1:
            own_qkv = qkv
        if t == 2:
            right = after(right, own_qkv)
        ways = [(0, passing)]
        if t:
            right = passing = net.along(right, 1)
            ways = [(-t, right)]
            if t <= (seq - 1) // 2:
                left = net.along(left, -1)
                ways.append((t, left))
        for by, value in ways:
            for page_at, x in ((core, value), (1 - core, net.sibling(value))):
                spot = jnp.stack([page_at, net.z_at(by)]).astype(jnp.int32)
                h_all, qkv = project(spot, x, gain[0], shift[0], w_qkv, b_qkv, h_all, qkv)
    h_all = h_all.reshape(2 * seq * rows, width)
    qkv = qkv.reshape(2, seq * rows, 3 * lanes)

    cot_two = jnp.concatenate([cot, net.sibling(cot)], axis=0)

    att_rows = min(512, rows)
    def to_tokens(value):
        blocks = value.reshape(seq, rows, lanes)
        sent = [pick(blocks, net.z_at(-s)) for s in range(1, seq)]
        got = [net.along(value, -s - 1) for s, value in enumerate(sent)]
        return jnp.concatenate([pick(blocks, z)] + got, axis=1)

    def to_heads(value):
        blocks = by_core(net, value[:rows], value[rows:])
        out = put(jnp.zeros((2, seq, rows, lanes), BF16), blocks[..., :lanes], z, 1)
        for s in range(1, seq):
            got = net.along(blocks[..., s * lanes : (s + 1) * lanes], s)
            out = put(out, got, net.z_at(-s), 1)
        return out.reshape(2, seq * rows, lanes)

    def turned(weight, by):
        twice = jnp.concatenate([weight, weight], axis=0)
        return lax.dynamic_slice_in_dim(twice, by * lanes, half, axis=0)

    o_self, lse_self, attended = [], [], []
    order = jnp.zeros((1,), jnp.int32)
    for k in range(2):
        order = after(order, o_self[0]) if k else order
        out, lse = self_fwd(order, qkv, att_rows, k)
        o_self.append(out)
        lse_self.append(lse)
        attended.append(to_tokens(out[0]))
    attended = jnp.concatenate(own_first(net, jnp.stack(attended)), axis=0)
    up_line = line_gather_held(net, after(up_parts, passing), 1, o_self[1])
    w_up = plane_gather(net, up_line).reshape(width, hidden // 2)
    mem_page = line_gather(net, mem, 0).reshape(-1, width)
    down_line = line_gather_held(net, after(ff_out, o_self[1]), 0, attended)
    w_down = plane_gather(net, down_line).reshape(hidden // 2, width)
    mem_all = jnp.concatenate([mem_page, net.sibling(mem_page)], axis=0)
    mem_rows = mem_page.shape[0]
    b_kv = jnp.concatenate([jnp.zeros((half,), F32), halves(bias[4])])
    kv_cross = (dot(mem_all, w_cross_kv) + b_kv).astype(BF16)
    kv_own, kv_other = kv_cross[:mem_rows], kv_cross[mem_rows:]


    def summed(rows_two, weight, dims=NN):
        sent = dot(rows_two[rows:], weight, dims).astype(BF16)
        back = net.sibling(sent)
        return dot(rows_two[:rows], weight, dims) + back.astype(F32)

    def both_pages(value):
        return jnp.concatenate([value, net.sibling(value)], axis=0)

    w_self_out = turned(w_self_out, z)
    x_in = tok.astype(F32)
    x_one = x_in + summed(attended, w_self_out) + bias[2]

    h_two = both_pages(layer_norm(x_one, gain[1], shift[1]))
    q_cross = (dot(h_two, w_cross_q) + halves(bias[3])).astype(BF16)
    oc_own, lse_own = cross_fwd(limit_own, q_cross[:rows], kv_own)
    oc_other, lse_other = cross_fwd(limit_other, q_cross[rows:], kv_other)
    o_cross = jnp.concatenate([oc_own, oc_other], axis=0)
    x_two = x_one + summed(o_cross, w_cross_out) + bias[5]

    h_three = both_pages(layer_norm(x_two, gain[2], shift[2]))
    pre_act = dot(h_three, w_up) + up_bias
    cdf = 0.5 + 0.5 * lax.erf(pre_act * (0.5**0.5))
    act = (pre_act * cdf).astype(BF16)
    layer_rows = (x_two + summed(act, w_down) + bias[6]).astype(BF16)

    slope = cdf + pre_act * (jnp.exp(-0.5 * pre_act * pre_act) * 0.3989422804014327)
    g_pre = (dot(cot_two, w_down, NT) * slope).astype(BF16)
    grad_down = dot(act, cot_two, TN).astype(BF16)
    grad_up = dot(h_three, g_pre, TN).astype(BF16)
    grad_up = after(grad_up, grad_down)
    part_down = plane_scatter(net, grad_down.reshape(chips, seq, ff_shard, width))
    part_up = plane_scatter(net, grad_up.reshape(chips, 2, seq, shard, hidden // 2))
    cot_wide = cot.astype(F32)
    back, d_gain2, d_shift2 = norm_back(x_two, gain[2], summed(g_pre, w_up, NT))
    g_two = cot_wide + back

    g_cross = both_pages(after(g_two.astype(BF16), grad_down, grad_up))
    grad_cross_out = dot(o_cross, g_cross, TN).astype(BF16)
    d_oc = dot(g_cross, w_cross_out, NT).astype(BF16)
    dq_own, dk_own, dv_own = cross_bwd(
        limit_own, q_cross[:rows], kv_own, d_oc[:rows], oc_own, lse_own
    )
    dq_other, dk_other, dv_other = cross_bwd(
        limit_other, q_cross[rows:], kv_other, d_oc[rows:], oc_other, lse_other
    )
    dq_cross = jnp.concatenate([dq_own, dq_other], axis=0)
    dq_cross = after(dq_cross, part_down)
    dkv_own = jnp.concatenate([dk_own, dv_own], axis=1)
    dkv_other = jnp.concatenate([dk_other, dv_other], axis=1)
    dkv_cross = jnp.concatenate([dkv_own, dkv_other], axis=0)
    grad_cross = jnp.concatenate(
        [dot(h_two, dq_cross, TN).astype(BF16), dot(mem_all, dkv_cross, TN).astype(BF16)], axis=1
    )
    part_cross = plane_scatter(net, grad_cross.reshape(chips, 2, seq, shard, 3 * half))
    mem_sent = dot(dkv_other, w_cross_kv, NT).astype(BF16)
    mem_grad = dot(dkv_own, w_cross_kv, NT) + net.sibling(mem_sent).astype(F32)
    back, d_gain1, d_shift1 = norm_back(x_one, gain[1], summed(dq_cross, w_cross_q, NT))
    g_one = g_two + back

    grad_memory = seq_scatter(mem_grad.reshape(seq, -1, width).astype(BF16))
    g_self = both_pages(after(g_one.astype(BF16), grad_cross))
    grad_self_out = turned(dot(attended, g_self, TN).astype(BF16), lax.rem(seq - z, seq))
    grad_outs = jnp.concatenate([grad_self_out, grad_cross_out], axis=1)
    part_outs = plane_scatter(net, grad_outs.reshape(chips, seq, shard, 2 * width))
    d_os = to_heads(dot(g_self, w_self_out, NT).astype(BF16))
    d_os = after(d_os, grad_outs, grad_memory)
    ff_rows = 2 * shard
    low_down = part_down.reshape(seq, 2, ff_shard // 2, width)
    low_down = jnp.concatenate([low_down[:, 0], low_down[:, 1]], axis=2)
    low_up = part_up.transpose(1, 0, 2, 3).reshape(seq, ff_rows, hidden // 2)
    sum_ff = seq_scatter(after(jnp.concatenate([low_up, low_down], axis=1), d_os))
    page_grads, d_hs = [], []
    for k in range(2):
        lse = after(lse_self[k], here) if k else lse_self[k]
        page_grad = self_bwd(qkv, d_os, o_self[k], lse, att_rows, k)[0]
        page_grads.append(page_grad)
        sides = w_qkv.reshape(2, half, 3 * lanes)
        there = dot(page_grad, pick(sides, 1 - core), NT).astype(BF16)
        here = dot(page_grad, pick(sides, core), NT) + net.sibling(there).astype(F32)
        d_hs.append(here)
    d_hs = [
        line_two_way_scatter(net, d_hs[k].reshape(seq, rows, half), () if k else (here,)) for k in range(2)
    ]
    own, other = own_first(net, jnp.stack(d_hs))
    other = net.sibling(other)
    d_h = jnp.concatenate(
        [jnp.where(core == 0, own, other), jnp.where(core == 0, other, own)], axis=1
    )
    sum_ff = after(sum_ff, d_hs[0])
    sum_up = sum_ff[:ff_rows].reshape(2, shard, hidden // 2)
    sum_down = sum_ff[ff_rows:]
    sum_down = jnp.concatenate([sum_down[:, :width], sum_down[:, width:]], axis=0)
    last = jnp.concatenate([part_cross[0], part_cross[1], part_outs], axis=2)
    last = seq_scatter(after(last, here))
    sum_outs = last[:, 6 * half :]
    sum_cross = jnp.stack([last[:, : 3 * half], last[:, 3 * half : 6 * half]])
    columns = jnp.concatenate([sum_up, sum_cross], axis=2)
    own, other = own_first(net, columns)
    other = net.sibling(other)
    sides = [jnp.where(core == k, own, other) for k in range(2)]

    def joined(at, count):
        two = jnp.stack([side[:, at : at + count] for side in sides], axis=1)
        return join_halves(two)

    sum_up = joined(0, hidden // 2)
    sum_cross = jnp.stack([joined(hidden // 2 + k * half, half) for k in range(3)])
    flat = after(jnp.concatenate(page_grads, axis=0), here, part_cross)
    back, _, _ = norm_back(x_in, gain[0], d_h)
    token_grad = g_one + back

    def spread(vector):
        split = vector.reshape(pages // 2, 1, width // pages)
        here = jnp.arange(2)[None, :, None] == core
        return jnp.where(here, split, 0.0).reshape(width)

    def spread_heads(vector):
        return lax.dynamic_update_slice_in_dim(jnp.zeros((width,), F32), vector, first, 0)

    sums_qkv = column_sum(flat)
    grad_qkv = dot(h_all, flat, TN)
    w_wide = w_qkv.astype(F32)
    by_row = (grad_qkv - shift[0][:, None] * sums_qkv) / gain[0][:, None]
    d_gain0 = jnp.sum(w_wide * by_row, axis=1)
    d_shift0 = jnp.sum(w_wide * sums_qkv, axis=1)
    up_sum = column_sum(g_pre).reshape(chips, 1, seq * ff_shard)
    up_sum = jnp.where(jnp.arange(2)[None, :, None] == core, up_sum, 0.0)
    vectors = jnp.stack(
        [
            d_gain0,
            d_gain1,
            d_gain2,
            d_shift0,
            d_shift1,
            d_shift2,
            spread_heads(sums_qkv[:lanes]),
            spread_heads(sums_qkv[2 * lanes :]),
            column_sum(g_one),
            spread(column_sum(dq_cross)),
            spread(column_sum(dkv_cross[:, half:])),
            column_sum(g_two),
            column_sum(cot_wide),
        ]
    )
    small = jnp.concatenate([vectors.T, up_sum.reshape(width, ff_shard // shard)], axis=1)
    small = jnp.pad(small, ((0, 0), (0, side - small.shape[1])))
    parts = jnp.concatenate([grad_qkv.astype(BF16), small.astype(BF16)], axis=1)
    parts = ring_scatter(net, parts.reshape(chips, 2, seq * shard, 3 * lanes + side))
    parts = parts.reshape(2, seq, shard, 3 * lanes + side)
    low = parts.astype(BF16)
    piece = jnp.zeros((2, seq, shard, 3 * lanes), BF16)
    piece = put(piece, pick(low, z, 1)[..., : 3 * lanes], z, 1)
    small = pick(parts, z, 1)[..., 3 * lanes :]
    for s in range(1, seq):
        got = net.along(pick(low, net.z_at(s), 1), s)
        piece = put(piece, got[..., : 3 * lanes], net.z_at(-s), 1)
        small += got[..., 3 * lanes :].astype(F32)
    own, other = own_first(net, piece)
    piece = by_core(net, own, net.sibling(other))
    sum_self = piece.reshape(2, seq, shard, 3, lanes).transpose(3, 2, 1, 0, 4)
    sum_self = sum_self.reshape(3, shard, width).astype(F32)
    own, other = own_first(net, small)
    small = own + net.sibling(other)
    vectors = small[:, :13].T
    return (
        layer_rows[None],
        token_grad[None],
        grad_memory[None],
        vectors[0:3],
        vectors[3:6],
        sum_self,
        sum_outs[:, :width],
        sum_cross,
        sum_outs[:, width:],
        sum_up,
        sum_down,
        vectors[6:13],
        small[:, 13 : 13 + ff_shard // shard].reshape(ff_shard),
    )


def solution(mesh):
    weight = P(AXES, None)
    return jax.shard_map(
        functools.partial(on_device, mesh=mesh),
        mesh=mesh,
        in_specs=(
            P("page", "seq", None),
            P("page", "seq", None),
            P("page", "seq", None),
            P("page"),
            P(None, AXES),
            P(None, AXES),
            P(None, AXES, None),
            weight,
            P(None, AXES, None),
            weight,
            weight,
            weight,
            P(None, AXES),
            P(AXES),
        ),
        out_specs=(
            P("page", "seq", None),
            P("page", "seq", None),
            P("page", "seq", None),
            P(None, AXES),
            P(None, AXES),
            P(None, AXES, None),
            weight,
            P(None, AXES, None),
            weight,
            weight,
            weight,
            P(None, AXES),
            P(AXES),
        ),
        check_vma=False,
    )
```

```python
import functools
import math

import jax
import jax.numpy as jnp
from jax import lax
from jax.experimental import pallas as pl
from jax.experimental.pallas import tpu as pltpu
from jax.sharding import PartitionSpec as P

HEADS = 16
HEAD_DIM = 64
VALID_HI = 588
VALID_LO = 140

NEGATIVE = -1e30
EPSILON = 1e-05
LOG2E = 1.4426950408889634
SCALING = HEAD_DIM ** (-0.5)
AXES = ("page", "seq")
F32 = jnp.float32
BF16 = jnp.bfloat16
NT = (((1,), (1,)), ((), ()))
NN = (((1,), (0,)), ((), ()))
TN = (((0,), (0,)), ((), ()))


def dot(a, b, dims=NN):
    return lax.dot_general(a, b, dims, preferred_element_type=F32)


def project_kernel(spot_ref, x_ref, gain_ref, shift_ref, w_ref, b_ref, h_in, qkv_in, h_ref, qkv_ref):
    del spot_ref, h_in, qkv_in
    x = x_ref[...].astype(F32)
    centered = x - jnp.mean(x, axis=-1, keepdims=True)
    scale = lax.rsqrt(jnp.mean(centered * centered, axis=-1, keepdims=True) + EPSILON)
    h = (centered * scale * gain_ref[...] + shift_ref[...]).astype(BF16)
    h_ref[0, 0] = h
    qkv_ref[0, 0] = (dot(h, w_ref[...]) + b_ref[...]).astype(BF16)


def project(spot, x, gain, shift, w_qkv, b_qkv, h_all, qkv):
    rows, width = x.shape
    wide = w_qkv.shape[1]
    block = min(256, rows)
    whole = lambda shape: pl.BlockSpec(shape, lambda i, n: (0, 0))
    return pl.pallas_call(
        project_kernel,
        grid_spec=pltpu.PrefetchScalarGridSpec(
            num_scalar_prefetch=1,
            grid=(rows // block,),
            in_specs=[
                pl.BlockSpec((block, width), lambda i, n: (i, 0)),
                whole((1, width)),
                whole((1, width)),
                whole((width, wide)),
                whole((1, wide)),
                pl.BlockSpec(memory_space=pl.ANY),
                pl.BlockSpec(memory_space=pl.ANY),
            ],
            out_specs=[
                pl.BlockSpec((1, 1, block, width), lambda i, n: (n[0], n[1], i, 0)),
                pl.BlockSpec((1, 1, block, wide), lambda i, n: (n[0], n[1], i, 0)),
            ],
        ),
        out_shape=[
            jax.ShapeDtypeStruct(h_all.shape, BF16),
            jax.ShapeDtypeStruct(qkv.shape, BF16),
        ],
        input_output_aliases={6: 0, 7: 1},
        compiler_params=pltpu.CompilerParams(vmem_limit_bytes=32 * 1024 * 1024),
        cost_estimate=pl.CostEstimate(
            flops=2 * rows * width * wide, bytes_accessed=4 * rows * width, transcendentals=0
        ),
    )(spot, x, gain[None], shift[None], w_qkv, b_qkv[None], h_all, qkv)


def self_fwd_kernel(order_ref, q_ref, kv_ref, o_ref, lse_ref, *, rows, width):
    del order_ref
    i = pl.program_id(1)
    heads = width // HEAD_DIM
    queries = [q_ref[0, :, h * HEAD_DIM : (h + 1) * HEAD_DIM] for h in range(heads)]
    ones = jnp.ones((16, rows), BF16)

    def step(j, carry, diagonal):
        at = pl.ds(pl.multiple_of(j * rows, rows), rows)
        keys_all = kv_ref[0, at, width : 2 * width]
        values_t = kv_ref[0, at, 2 * width : 3 * width].T
        out = []
        for h in range(heads):
            run_max, acc = carry[h]
            lanes = slice(h * HEAD_DIM, (h + 1) * HEAD_DIM)
            scores = dot(keys_all[:, lanes], queries[h], NT) * (SCALING * LOG2E)
            if diagonal:
                place_k = lax.broadcasted_iota(jnp.int32, (rows, rows), 0)
                place_q = lax.broadcasted_iota(jnp.int32, (rows, rows), 1)
                scores = jnp.where(place_k <= place_q, scores, NEGATIVE)
            new_max = jnp.maximum(run_max, jnp.max(scores, axis=0, keepdims=True))
            probs = jnp.exp2(scores - new_max).astype(BF16)
            wide = jnp.concatenate([values_t[lanes], ones], axis=0)
            out.append((new_max, acc * jnp.exp2(run_max - new_max) + dot(wide, probs)))
        return tuple(out)

    start = tuple(
        (jnp.full((1, rows), NEGATIVE, F32), jnp.zeros((HEAD_DIM + 16, rows), F32))
        for _ in range(heads)
    )
    carry = lax.fori_loop(0, i, lambda j, c: step(j, c, False), start)
    carry = step(i, carry, True)
    outs = []
    for h in range(heads):
        run_max, acc = carry[h]
        total = acc[HEAD_DIM : HEAD_DIM + 1]
        outs.append(acc[:HEAD_DIM] / total)
        lse_ref[0, h] = run_max + jnp.log2(total)
    o_ref[0] = jnp.concatenate(outs, axis=0).T.astype(BF16)


def self_fwd(order, qkv, rows, page):
    length, three = qkv.shape[1:]
    width = three // 3
    heads = width // HEAD_DIM
    cost = heads * length * length * HEAD_DIM * 2
    return pl.pallas_call(
        functools.partial(self_fwd_kernel, rows=rows, width=width),
        grid=(1, length // rows),
        in_specs=[
            pl.BlockSpec(memory_space=pltpu.SMEM),
            pl.BlockSpec((1, rows, three), lambda p, i: (page, i, 0)),
            pl.BlockSpec((1, length, three), lambda p, i: (page, 0, 0)),
        ],
        out_specs=[
            pl.BlockSpec((1, rows, width), lambda p, i: (0, i, 0)),
            pl.BlockSpec((1, heads, 1, rows), lambda p, i: (0, 0, 0, i)),
        ],
        out_shape=[
            jax.ShapeDtypeStruct((1, length, width), BF16),
            jax.ShapeDtypeStruct((1, heads, 1, length), F32),
        ],
        compiler_params=pltpu.CompilerParams(vmem_limit_bytes=48 * 1024 * 1024),
        cost_estimate=pl.CostEstimate(
            flops=2 * cost, bytes_accessed=4 * qkv.size, transcendentals=cost // 256
        ),
    )(order, qkv, qkv)


def self_bwd_kernel(q_ref, kv_ref, do_ref, o_ref, lse_ref, out_ref, dk_acc, dv_acc, *, rows, width):
    i = pl.program_id(1)
    heads = width // HEAD_DIM

    @pl.when(i == 0)
    def _():
        dk_acc[...] = jnp.zeros_like(dk_acc)
        dv_acc[...] = jnp.zeros_like(dv_acc)

    q_all = q_ref[0, :, :width]
    do_all = do_ref[0]
    prod = (do_all.astype(F32) * o_ref[0].astype(F32)).T
    per_head = [slice(h * HEAD_DIM, (h + 1) * HEAD_DIM) for h in range(heads)]
    deltas = [jnp.sum(prod[s], axis=0, keepdims=True) for s in per_head]

    def step(j, carry, diagonal):
        at = pl.ds(pl.multiple_of(j * rows, rows), rows)
        k_all = kv_ref[0, at, width : 2 * width]
        v_all = kv_ref[0, at, 2 * width : 3 * width]
        k_t = k_all.T
        new, dks, dvs = [], [], []
        for h in range(heads):
            s = per_head[h]
            scores = dot(k_all[:, s], q_all[:, s], NT) * (SCALING * LOG2E)
            probs = jnp.exp2(scores - lse_ref[0, h])
            if diagonal:
                place_k = lax.broadcasted_iota(jnp.int32, (rows, rows), 0)
                place_q = lax.broadcasted_iota(jnp.int32, (rows, rows), 1)
                probs = jnp.where(place_k <= place_q, probs, 0.0)
            d_probs = dot(v_all[:, s], do_all[:, s], NT)
            d_scores = (probs * (d_probs - deltas[h])).astype(BF16)
            dvs.append(dot(probs.astype(BF16), do_all[:, s]))
            dks.append(dot(d_scores, q_all[:, s]))
            new.append(carry[h] + dot(k_t[s], d_scores))
        dk_acc[at, :] += jnp.concatenate(dks, axis=1)
        dv_acc[at, :] += jnp.concatenate(dvs, axis=1)
        return tuple(new)

    start = tuple(jnp.zeros((HEAD_DIM, rows), F32) for _ in range(heads))
    carry = lax.fori_loop(0, i, lambda j, c: step(j, c, False), start)
    carry = step(i, carry, True)
    dq = (jnp.concatenate(carry, axis=0) * SCALING).T.astype(BF16)
    out_ref[0, pl.ds(pl.multiple_of(i * rows, rows), rows), :width] = dq

    @pl.when(i == pl.num_programs(1) - 1)
    def _():
        out_ref[0, :, width : 2 * width] = (dk_acc[...] * SCALING).astype(BF16)
        out_ref[0, :, 2 * width :] = dv_acc[...].astype(BF16)


def self_bwd(qkv, d_out, out, lse, rows, page):
    length, three = qkv.shape[1:]
    width = three // 3
    heads = width // HEAD_DIM
    cost = heads * length * length * HEAD_DIM * 5
    return pl.pallas_call(
        functools.partial(self_bwd_kernel, rows=rows, width=width),
        grid=(1, length // rows),
        in_specs=[
            pl.BlockSpec((1, rows, three), lambda p, i: (page, i, 0)),
            pl.BlockSpec((1, length, three), lambda p, i: (page, 0, 0)),
            pl.BlockSpec((1, rows, width), lambda p, i: (page, i, 0)),
            pl.BlockSpec((1, rows, width), lambda p, i: (0, i, 0)),
            pl.BlockSpec((1, heads, 1, rows), lambda p, i: (0, 0, 0, i)),
        ],
        out_specs=pl.BlockSpec((1, length, three), lambda p, i: (0, 0, 0)),
        out_shape=jax.ShapeDtypeStruct((1, length, three), BF16),
        scratch_shapes=[pltpu.VMEM((length, width), F32), pltpu.VMEM((length, width), F32)],
        compiler_params=pltpu.CompilerParams(vmem_limit_bytes=48 * 1024 * 1024),
        cost_estimate=pl.CostEstimate(
            flops=2 * cost, bytes_accessed=6 * qkv.size, transcendentals=cost // 640
        ),
    )(qkv, qkv, d_out, out, lse)


def cross_fwd_kernel(limit_ref, q_ref, k_ref, v_ref, o_ref, lse_ref):
    limit = limit_ref[0]
    rows, mem = q_ref.shape[0], k_ref.shape[0]
    valid = lax.broadcasted_iota(jnp.int32, (mem, rows), 0) < limit
    values_t = v_ref[...].T
    ones = jnp.ones((16, mem), BF16)
    outs = []
    for h in range(2):
        s = slice(h * HEAD_DIM, (h + 1) * HEAD_DIM)
        scores = dot(k_ref[:, s], q_ref[:, s], NT) * (SCALING * LOG2E)
        scores = jnp.where(valid, scores, NEGATIVE)
        top = jnp.max(scores, axis=0, keepdims=True)
        probs = jnp.exp2(scores - top).astype(BF16)
        acc = dot(jnp.concatenate([values_t[s], ones], axis=0), probs)
        total = acc[HEAD_DIM : HEAD_DIM + 1]
        outs.append(acc[:HEAD_DIM] / total)
        lse_ref[0, h : h + 1] = top + jnp.log2(total)
    o_ref[...] = jnp.concatenate(outs, axis=0).T.astype(BF16)


def cross_fwd(limit, q, kv):
    rows, width = q.shape
    mem = kv.shape[0]
    pairs = width // (2 * HEAD_DIM)
    wide = 2 * HEAD_DIM
    cost = width * rows * mem * 2
    return pl.pallas_call(
        cross_fwd_kernel,
        grid_spec=pltpu.PrefetchScalarGridSpec(
            num_scalar_prefetch=1,
            grid=(pairs,),
            in_specs=[
                pl.BlockSpec((rows, wide), lambda p, n: (0, p)),
                pl.BlockSpec((mem, wide), lambda p, n: (0, p)),
                pl.BlockSpec((mem, wide), lambda p, n: (0, p + pairs)),
            ],
            out_specs=[
                pl.BlockSpec((rows, wide), lambda p, n: (0, p)),
                pl.BlockSpec((1, 2, rows), lambda p, n: (p, 0, 0)),
            ],
        ),
        out_shape=[
            jax.ShapeDtypeStruct((rows, width), BF16),
            jax.ShapeDtypeStruct((pairs, 2, rows), F32),
        ],
        compiler_params=pltpu.CompilerParams(vmem_limit_bytes=48 * 1024 * 1024),
        cost_estimate=pl.CostEstimate(
            flops=2 * cost, bytes_accessed=4 * (q.size + kv.size), transcendentals=cost // 128
        ),
    )(limit, q, kv, kv)


def cross_bwd_kernel(limit_ref, q_ref, k_ref, v_ref, do_ref, o_ref, lse_ref, dq_ref, dk_ref, dv_ref):
    limit = limit_ref[0]
    rows, mem = q_ref.shape[0], k_ref.shape[0]
    valid = lax.broadcasted_iota(jnp.int32, (mem, rows), 0) < limit
    k_t = k_ref[...].T
    prod = (do_ref[...].astype(F32) * o_ref[...].astype(F32)).T
    dqs, dks, dvs = [], [], []
    for h in range(2):
        s = slice(h * HEAD_DIM, (h + 1) * HEAD_DIM)
        delta = jnp.sum(prod[s], axis=0, keepdims=True)
        scores = dot(k_ref[:, s], q_ref[:, s], NT) * (SCALING * LOG2E)
        scores = jnp.where(valid, scores, NEGATIVE)
        probs = jnp.exp2(scores - lse_ref[0, h : h + 1])
        d_probs = dot(v_ref[:, s], do_ref[:, s], NT)
        d_scores = (probs * (d_probs - delta)).astype(BF16)
        dvs.append(dot(probs.astype(BF16), do_ref[:, s]))
        dks.append(dot(d_scores, q_ref[:, s]))
        dqs.append(dot(k_t[s], d_scores))
    dq_ref[...] = (jnp.concatenate(dqs, axis=0) * SCALING).T.astype(BF16)
    dk_ref[...] = (jnp.concatenate(dks, axis=1) * SCALING).astype(BF16)
    dv_ref[...] = jnp.concatenate(dvs, axis=1).astype(BF16)


def cross_bwd(limit, q, kv, d_out, out, lse):
    rows, width = q.shape
    mem = kv.shape[0]
    pairs = width // (2 * HEAD_DIM)
    wide = 2 * HEAD_DIM
    cost = width * rows * mem * 5
    token_block = pl.BlockSpec((rows, wide), lambda p, n: (0, p))
    memory_block = pl.BlockSpec((mem, wide), lambda p, n: (0, p))
    return pl.pallas_call(
        cross_bwd_kernel,
        grid_spec=pltpu.PrefetchScalarGridSpec(
            num_scalar_prefetch=1,
            grid=(pairs,),
            in_specs=[
                token_block,
                memory_block,
                pl.BlockSpec((mem, wide), lambda p, n: (0, p + pairs)),
                token_block,
                token_block,
                pl.BlockSpec((1, 2, rows), lambda p, n: (p, 0, 0)),
            ],
            out_specs=[token_block, memory_block, memory_block],
        ),
        out_shape=[
            jax.ShapeDtypeStruct((rows, width), BF16),
            jax.ShapeDtypeStruct((mem, width), BF16),
            jax.ShapeDtypeStruct((mem, width), BF16),
        ],
        compiler_params=pltpu.CompilerParams(vmem_limit_bytes=48 * 1024 * 1024),
        cost_estimate=pl.CostEstimate(
            flops=2 * cost, bytes_accessed=6 * (q.size + kv.size), transcendentals=cost // 320
        ),
    )(limit, q, kv, kv, d_out, out, lse)


def gray(n):
    return n ^ (n >> 1)


class Net:
    def __init__(self, mesh):
        self.pages, self.seq = mesh.shape["page"], mesh.shape["seq"]
        self.chips = self.pages // 2
        page = lax.axis_index("page")
        self.core = lax.rem(page, 2)
        self.chip = lax.div(page, 2)
        self.z = lax.axis_index("seq")
        place = self.chip
        shift = 1
        while (self.chips - 1) >> shift:
            place = place ^ (self.chip >> shift)
            shift += 1
        self.place = place
        where = {gray(j): j for j in range(self.chips)}

        def index(chip, core, z):
            return (chip * 2 + core) * self.seq + z

        everyone = [
            (chip, core, z)
            for chip in range(self.chips)
            for core in range(2)
            for z in range(self.seq)
        ]
        self.planes = [
            [index(chip, core, z) for chip in range(self.chips)]
            for core in range(2)
            for z in range(self.seq)
        ]
        self.pair_map = [(index(h, c, z), index(h, 1 - c, z)) for h, c, z in everyone]
        self.line_map = [
            [(index(h, c, z), index(h, c, (z + s) % self.seq)) for h, c, z in everyone]
            for s in range(self.seq)
        ]
        self.ring_map = {
            way: [
                (index(h, c, z), index(gray((where[h] + way) % self.chips), c, z))
                for h, c, z in everyone
            ]
            for way in (1, -1)
        }

    def sibling(self, value):
        return lax.ppermute(value, AXES, self.pair_map)

    def along(self, value, by):
        return lax.ppermute(value, AXES, self.line_map[by % self.seq])

    def around(self, value, way):
        return lax.ppermute(value, AXES, self.ring_map[way])

    def chip_at(self, by):
        j = lax.rem(self.place + by + self.chips, self.chips)
        return j ^ (j >> 1)

    def z_at(self, by):
        return lax.rem(self.z + by + self.seq, self.seq)


def put(buffer, piece, index, axis):
    return lax.dynamic_update_slice_in_dim(buffer, jnp.expand_dims(piece, axis), index, axis)


def pick(buffer, index, axis=0):
    return lax.dynamic_index_in_dim(buffer, index, axis, keepdims=False)


def line_pieces(net, piece):
    yield 0, piece
    right, left = piece, piece
    for t in range(1, net.seq // 2 + 1):
        right = net.along(right, 1)
        yield -t, right
        if t <= (net.seq - 1) // 2:
            left = net.along(left, -1)
            yield t, left


def line_gather(net, piece, axis):
    out = jnp.zeros(piece.shape[:axis] + (net.seq,) + piece.shape[axis:], piece.dtype)
    for by, got in line_pieces(net, piece):
        out = put(out, got, net.z_at(by), axis)
    return out


def line_gather_held(net, piece, axis, *others):
    out = put(jnp.zeros(piece.shape[:axis] + (net.seq,) + piece.shape[axis:], piece.dtype), piece, net.z, axis)
    for s in range(1, net.seq):
        out = put(out, after(net.along(piece, s), *others), net.z_at(-s), axis)
    return out


def ring_gather(net, piece):
    half = piece.shape[0] // 2
    out = put(jnp.zeros((net.chips,) + piece.shape, piece.dtype), piece, net.chip, 0)
    right, left = piece, piece
    for t in range(1, net.chips // 2):
        right, left = net.around(right, 1), net.around(left, -1)
        out = put(out, right, net.chip_at(-t), 0)
        out = put(out, left, net.chip_at(t), 0)
    far = net.chip_at(net.chips // 2)
    right, left = net.around(right[:half], 1), net.around(left[half:], -1)
    return put(out, jnp.concatenate([right, left], axis=0), far, 0)


def ring_scatter(net, parts):
    half = parts.shape[1] // 2
    steps = net.chips // 2
    far = pick(parts, net.chip_at(steps))
    right, left = net.around(far[:half], 1), net.around(far[half:], -1)
    for t in range(1, steps):
        k = steps - t
        mine = pick(parts, net.chip_at(k))
        if t == 1:
            first = mine[:half].astype(F32) + right.astype(F32)
            sent = jnp.concatenate([first.astype(BF16), mine[half:]], axis=0)
        else:
            sent = (mine.astype(F32) + right.astype(F32)).astype(BF16)
        mine = pick(parts, net.chip_at(-k))
        if t == 1:
            first = mine[half:].astype(F32) + left.astype(F32)
            back = jnp.concatenate([mine[:half], first.astype(BF16)], axis=0)
        else:
            back = (mine.astype(F32) + left.astype(F32)).astype(BF16)
        right, left = net.around(sent, 1), net.around(back, -1)
    return pick(parts, net.chip).astype(F32) + right.astype(F32) + left.astype(F32)


def line_scatter(net, parts, axis):
    low = parts.astype(BF16)
    sent = [pick(low, net.z_at(s), axis) for s in range(1, net.seq)]
    got = [net.along(value, s + 1) for s, value in enumerate(sent)]
    return pick(parts, net.z, axis).astype(F32) + sum(value.astype(F32) for value in got)


def own_first(net, value):
    return pick(value, net.core), pick(value, 1 - net.core)


def by_core(net, own, other):
    return jnp.where(net.core == 0, jnp.stack([own, other]), jnp.stack([other, own]))


def plane_gather(net, piece):
    return lax.all_gather(piece, AXES, axis=0, axis_index_groups=net.planes)


def plane_scatter(net, parts):
    flat = parts.reshape(-1, parts.shape[-1])
    mine = lax.psum_scatter(
        flat, AXES, scatter_dimension=0, axis_index_groups=net.planes, tiled=True
    )
    return mine.reshape(parts.shape[1:])


def seq_scatter(parts):
    flat = parts.reshape(-1, parts.shape[-1])
    mine = lax.psum_scatter(flat, "seq", scatter_dimension=0, tiled=True)
    return mine.reshape(parts.shape[1:]).astype(F32)


def after(value, *others):
    for other in others:
        element = lax.optimization_barrier(other)[(0,) * other.ndim].astype(F32)
        value = value + jnp.minimum(jnp.abs(element), 0.0).astype(value.dtype)
    return value


def scatter_columns(net, grad, rows):
    parts = grad.reshape(net.chips, 2, net.seq, rows, grad.shape[-1])
    mine = line_scatter(net, plane_scatter(net, parts), 1)
    own, other = own_first(net, mine)
    return jnp.moveaxis(by_core(net, own, net.sibling(other)), 0, 1)


def scatter_rows(net, grad, rows):
    parts = grad.reshape(net.chips, net.seq, rows, grad.shape[-1])
    return line_scatter(net, plane_scatter(net, parts), 0)


def line_two_way_scatter(net, parts, hold=()):
    total = pick(parts, net.z)
    for way, far in ((1, net.seq // 2), (-1, (net.seq - 1) // 2)):
        got = None
        for by in range(far, 0, -1):
            mine = pick(parts, net.z_at(way * by))
            sent = mine.astype(BF16) if got is None else after((mine + got).astype(BF16), *hold)
            got = net.along(sent, way).astype(F32)
        if got is not None:
            total += got
    return total


def norm_parts(values):
    centered = values - jnp.mean(values, axis=-1, keepdims=True)
    scale = lax.rsqrt(jnp.mean(centered * centered, axis=-1, keepdims=True) + EPSILON)
    return centered * scale, scale


def layer_norm(values, gain, shift):
    return (norm_parts(values)[0] * gain + shift).astype(BF16)


def norm_back(values, gain, upstream):
    normed, scale = norm_parts(values)
    scaled = upstream * gain
    mean_g = jnp.mean(scaled, axis=-1, keepdims=True)
    mean_gn = jnp.mean(scaled * normed, axis=-1, keepdims=True)
    grad = (scaled - mean_g - normed * mean_gn) * scale
    return grad, jnp.sum(upstream * normed, axis=0), jnp.sum(upstream, axis=0)


def column_sum(values):
    return jnp.sum(values.astype(F32), axis=0)


def on_device(
    tokens,
    memory,
    cotangent,
    res_flag,
    ln_gain,
    ln_bias,
    self_in,
    self_out,
    cross_in,
    cross_out,
    ff_in,
    ff_out,
    proj_bias,
    ff_bias,
    *,
    mesh,
):
    net = Net(mesh)
    core, z = net.core, net.z
    rows, width = tokens.shape[1], tokens.shape[2]
    seq, chips, pages = net.seq, net.chips, net.pages
    shard = self_in.shape[1]
    hidden = ff_in.shape[1]
    ff_shard = ff_out.shape[0]
    lanes = width // (2 * seq)
    half = width // 2
    tok, mem, cot = tokens[0], memory[0], cotangent[0]

    def halves(vector):
        return pick(vector.reshape(pages // 2, 2, width // pages), core, 1).reshape(half)

    def column_halves(weight):
        lead, columns = weight.shape[:-1], weight.shape[-1]
        split = weight.reshape(lead + (pages // 2, 2, columns // pages))
        return jnp.moveaxis(split, -2, -3).reshape(lead + (2, columns // 2))

    def join_halves(weight):
        lead, columns = weight.shape[:-2], weight.shape[-1] * 2
        split = weight.reshape(lead + (2, pages // 2, columns // pages))
        return jnp.moveaxis(split, -3, -2).reshape(lead + (columns,))

    side = 128
    small = jnp.concatenate(
        [
            ln_gain.T,
            ln_bias.T,
            proj_bias.T,
            jnp.broadcast_to(res_flag.astype(BF16)[:, None], (shard, 1)),
            ff_bias.reshape(shard, ff_shard // shard),
        ],
        axis=1,
    )
    small = jnp.pad(small, ((0, 0), (0, side - small.shape[1])))
    blocks = self_in.reshape(3, shard, seq, 2, lanes).transpose(3, 2, 1, 0, 4)
    blocks = blocks.reshape(2, seq, shard, 3 * lanes)
    small = jnp.broadcast_to(small, (2, seq, shard, side))
    blocks = jnp.concatenate([blocks, small], axis=3)
    own, other = own_first(net, blocks)
    blocks = by_core(net, own, net.sibling(other))
    piece = jnp.zeros_like(blocks)
    piece = put(piece, pick(blocks, z, 1), z, 1)
    for s in range(1, seq):
        piece = put(piece, net.along(pick(blocks, net.z_at(s), 1), s), net.z_at(-s), 1)
    qkv_line = piece
    w_wide = ring_gather(net, piece).reshape(width, 3 * lanes + side)
    w_qkv = w_wide[:, : 3 * lanes]
    small = w_wide[:, 3 * lanes :].astype(F32)
    vectors = small[:, :13].T
    gain, shift, bias = vectors[0:3], vectors[3:6], vectors[6:13]
    flags = small[:, 13].reshape(pages, seq * shard)[:, 0]
    up_bias = small[:, 14 : 14 + ff_shard // shard].reshape(chips, 2, seq * ff_shard)
    up_bias = pick(up_bias, core, 1).reshape(hidden // 2)
    page = lax.axis_index("page")

    def limit_of(which):
        return jnp.where(pick(flags, which) > 0.5, VALID_HI, VALID_LO).astype(jnp.int32).reshape(1)

    limit_own, limit_other = limit_of(page), limit_of(page ^ 1)

    limit_own, limit_other = limit_of(page), limit_of(page ^ 1)
    first = (2 * z + core) * lanes
    b_qkv = jnp.concatenate(
        [
            lax.dynamic_slice_in_dim(bias[0], first, lanes),
            jnp.zeros((lanes,), F32),
            lax.dynamic_slice_in_dim(bias[1], first, lanes),
        ]
    )

    cross_halves = column_halves(cross_in).transpose(2, 1, 0, 3).reshape(2, shard, 3 * half)
    column_parts = jnp.concatenate([cross_halves, column_halves(ff_in).transpose(1, 0, 2)], axis=2)
    own, other = own_first(net, column_parts)
    column_parts = by_core(net, own, net.sibling(other))
    cross_parts, up_parts = column_parts[:, :, : 3 * half], column_parts[:, :, 3 * half :]
    bundle = jnp.concatenate([cross_parts[0], cross_parts[1], self_out, cross_out], axis=1)
    bundle_line = line_gather(net, after(bundle, qkv_line), 0)
    bundle = plane_gather(net, bundle_line)

    def rows_of(at, columns):
        two = [bundle[..., c * 3 * half + at : c * 3 * half + at + columns] for c in range(2)]
        return jnp.stack(two, axis=1).reshape(width, columns)

    w_cross_q, w_cross_kv = rows_of(0, half), rows_of(half, width)
    w_self_out = bundle[..., 6 * half : 6 * half + width].reshape(half, width)
    w_cross_out = bundle[..., 6 * half + width :].reshape(half, width)
    h_all = jnp.zeros((2, seq, rows, width), BF16)
    qkv = jnp.zeros((2, seq, rows, 3 * lanes), BF16)
    right = left = passing = after(tok, qkv_line)
    for t in range(seq // 2 + 1):
        if t == 1:
            own_qkv = qkv
        if t == 2:
            right = after(right, own_qkv)
        ways = [(0, passing)]
        if t:
            right = passing = net.along(right, 1)
            ways = [(-t, right)]
            if t <= (seq - 1) // 2:
                left = net.along(left, -1)
                ways.append((t, left))
        for by, value in ways:
            for page_at, x in ((core, value), (1 - core, net.sibling(value))):
                spot = jnp.stack([page_at, net.z_at(by)]).astype(jnp.int32)
                h_all, qkv = project(spot, x, gain[0], shift[0], w_qkv, b_qkv, h_all, qkv)
    h_all = h_all.reshape(2 * seq * rows, width)
    qkv = qkv.reshape(2, seq * rows, 3 * lanes)

    cot_two = jnp.concatenate([cot, net.sibling(cot)], axis=0)

    att_rows = min(512, rows)
    def to_tokens(value):
        blocks = value.reshape(seq, rows, lanes)
        sent = [pick(blocks, net.z_at(-s)) for s in range(1, seq)]
        got = [net.along(value, -s - 1) for s, value in enumerate(sent)]
        return jnp.concatenate([pick(blocks, z)] + got, axis=1)

    def to_heads(value):
        blocks = by_core(net, value[:rows], value[rows:])
        out = put(jnp.zeros((2, seq, rows, lanes), BF16), blocks[..., :lanes], z, 1)
        for s in range(1, seq):
            got = net.along(blocks[..., s * lanes : (s + 1) * lanes], s)
            out = put(out, got, net.z_at(-s), 1)
        return out.reshape(2, seq * rows, lanes)

    def turned(weight, by):
        twice = jnp.concatenate([weight, weight], axis=0)
        return lax.dynamic_slice_in_dim(twice, by * lanes, half, axis=0)

    o_self, lse_self, attended = [], [], []
    order = jnp.zeros((1,), jnp.int32)
    for k in range(2):
        order = after(order, o_self[0]) if k else order
        out, lse = self_fwd(order, qkv, math.gcd(1024, seq * rows), k)
        o_self.append(out)
        lse_self.append(lse)
        attended.append(to_tokens(out[0]))
    attended = jnp.concatenate(own_first(net, jnp.stack(attended)), axis=0)
    up_line = line_gather_held(net, after(up_parts, passing), 1, o_self[1])
    w_up = plane_gather(net, up_line).reshape(width, hidden // 2)
    mem_page = line_gather(net, mem, 0).reshape(-1, width)
    down_line = line_gather_held(net, after(ff_out, o_self[1]), 0, attended)
    w_down = plane_gather(net, down_line).reshape(hidden // 2, width)
    mem_all = jnp.concatenate([mem_page, net.sibling(mem_page)], axis=0)
    mem_rows = mem_page.shape[0]
    b_kv = jnp.concatenate([jnp.zeros((half,), F32), halves(bias[4])])
    kv_cross = (dot(mem_all, w_cross_kv) + b_kv).astype(BF16)
    kv_own, kv_other = kv_cross[:mem_rows], kv_cross[mem_rows:]


    def summed(rows_two, weight, dims=NN):
        sent = dot(rows_two[rows:], weight, dims).astype(BF16)
        back = net.sibling(sent)
        return dot(rows_two[:rows], weight, dims) + back.astype(F32)

    def both_pages(value):
        return jnp.concatenate([value, net.sibling(value)], axis=0)

    w_self_out = turned(w_self_out, z)
    x_in = tok.astype(F32)
    x_one = x_in + summed(attended, w_self_out) + bias[2]

    h_two = both_pages(layer_norm(x_one, gain[1], shift[1]))
    q_cross = (dot(h_two, w_cross_q) + halves(bias[3])).astype(BF16)
    oc_own, lse_own = cross_fwd(limit_own, q_cross[:rows], kv_own)
    oc_other, lse_other = cross_fwd(limit_other, q_cross[rows:], kv_other)
    o_cross = jnp.concatenate([oc_own, oc_other], axis=0)
    x_two = x_one + summed(o_cross, w_cross_out) + bias[5]

    h_three = both_pages(layer_norm(x_two, gain[2], shift[2]))
    pre_act = dot(h_three, w_up) + up_bias
    cdf = 0.5 + 0.5 * lax.erf(pre_act * (0.5**0.5))
    act = (pre_act * cdf).astype(BF16)
    layer_rows = (x_two + summed(act, w_down) + bias[6]).astype(BF16)

    slope = cdf + pre_act * (jnp.exp(-0.5 * pre_act * pre_act) * 0.3989422804014327)
    g_pre = (dot(cot_two, w_down, NT) * slope).astype(BF16)
    grad_down = dot(act, cot_two, TN).astype(BF16)
    grad_up = dot(h_three, g_pre, TN).astype(BF16)
    grad_up = after(grad_up, grad_down)
    part_down = plane_scatter(net, grad_down.reshape(chips, seq, ff_shard, width))
    part_up = plane_scatter(net, grad_up.reshape(chips, 2, seq, shard, hidden // 2))
    cot_wide = cot.astype(F32)
    back, d_gain2, d_shift2 = norm_back(x_two, gain[2], summed(g_pre, w_up, NT))
    g_two = cot_wide + back

    g_cross = both_pages(after(g_two.astype(BF16), grad_down, grad_up))
    grad_cross_out = dot(o_cross, g_cross, TN).astype(BF16)
    d_oc = dot(g_cross, w_cross_out, NT).astype(BF16)
    dq_own, dk_own, dv_own = cross_bwd(
        limit_own, q_cross[:rows], kv_own, d_oc[:rows], oc_own, lse_own
    )
    dq_other, dk_other, dv_other = cross_bwd(
        limit_other, q_cross[rows:], kv_other, d_oc[rows:], oc_other, lse_other
    )
    dq_cross = jnp.concatenate([dq_own, dq_other], axis=0)
    dq_cross = after(dq_cross, part_down)
    dkv_own = jnp.concatenate([dk_own, dv_own], axis=1)
    dkv_other = jnp.concatenate([dk_other, dv_other], axis=1)
    dkv_cross = jnp.concatenate([dkv_own, dkv_other], axis=0)
    grad_cross = jnp.concatenate(
        [dot(h_two, dq_cross, TN).astype(BF16), dot(mem_all, dkv_cross, TN).astype(BF16)], axis=1
    )
    part_cross = plane_scatter(net, grad_cross.reshape(chips, 2, seq, shard, 3 * half))
    mem_sent = dot(dkv_other, w_cross_kv, NT).astype(BF16)
    mem_grad = dot(dkv_own, w_cross_kv, NT) + net.sibling(mem_sent).astype(F32)
    back, d_gain1, d_shift1 = norm_back(x_one, gain[1], summed(dq_cross, w_cross_q, NT))
    g_one = g_two + back

    grad_memory = seq_scatter(mem_grad.reshape(seq, -1, width).astype(BF16))
    g_self = both_pages(after(g_one.astype(BF16), grad_cross))
    grad_self_out = turned(dot(attended, g_self, TN).astype(BF16), lax.rem(seq - z, seq))
    grad_outs = jnp.concatenate([grad_self_out, grad_cross_out], axis=1)
    part_outs = plane_scatter(net, grad_outs.reshape(chips, seq, shard, 2 * width))
    d_os = to_heads(dot(g_self, w_self_out, NT).astype(BF16))
    d_os = after(d_os, grad_outs, grad_memory)
    ff_rows = 2 * shard
    low_down = part_down.reshape(seq, 2, ff_shard // 2, width)
    low_down = jnp.concatenate([low_down[:, 0], low_down[:, 1]], axis=2)
    low_up = part_up.transpose(1, 0, 2, 3).reshape(seq, ff_rows, hidden // 2)
    sum_ff = seq_scatter(after(jnp.concatenate([low_up, low_down], axis=1), d_os))
    page_grads, d_hs = [], []
    for k in range(2):
        lse = after(lse_self[k], here) if k else lse_self[k]
        page_grad = self_bwd(qkv, d_os, o_self[k], lse, att_rows, k)[0]
        page_grads.append(page_grad)
        sides = w_qkv.reshape(2, half, 3 * lanes)
        there = dot(page_grad, pick(sides, 1 - core), NT).astype(BF16)
        here = dot(page_grad, pick(sides, core), NT) + net.sibling(there).astype(F32)
        d_hs.append(here)
    d_hs = [
        line_two_way_scatter(net, d_hs[k].reshape(seq, rows, half), () if k else (here,)) for k in range(2)
    ]
    own, other = own_first(net, jnp.stack(d_hs))
    other = net.sibling(other)
    d_h = jnp.concatenate(
        [jnp.where(core == 0, own, other), jnp.where(core == 0, other, own)], axis=1
    )
    sum_ff = after(sum_ff, d_hs[0])
    sum_up = sum_ff[:ff_rows].reshape(2, shard, hidden // 2)
    sum_down = sum_ff[ff_rows:]
    sum_down = jnp.concatenate([sum_down[:, :width], sum_down[:, width:]], axis=0)
    last = jnp.concatenate([part_cross[0], part_cross[1], part_outs], axis=2)
    last = seq_scatter(after(last, here))
    sum_outs = last[:, 6 * half :]
    sum_cross = jnp.stack([last[:, : 3 * half], last[:, 3 * half : 6 * half]])
    columns = jnp.concatenate([sum_up, sum_cross], axis=2)
    own, other = own_first(net, columns)
    other = net.sibling(other)
    sides = [jnp.where(core == k, own, other) for k in range(2)]

    def joined(at, count):
        two = jnp.stack([side[:, at : at + count] for side in sides], axis=1)
        return join_halves(two)

    sum_up = joined(0, hidden // 2)
    sum_cross = jnp.stack([joined(hidden // 2 + k * half, half) for k in range(3)])
    flat = after(jnp.concatenate(page_grads, axis=0), here, part_cross)
    back, _, _ = norm_back(x_in, gain[0], d_h)
    token_grad = g_one + back

    def spread(vector):
        split = vector.reshape(pages // 2, 1, width // pages)
        here = jnp.arange(2)[None, :, None] == core
        return jnp.where(here, split, 0.0).reshape(width)

    def spread_heads(vector):
        return lax.dynamic_update_slice_in_dim(jnp.zeros((width,), F32), vector, first, 0)

    sums_qkv = column_sum(flat)
    grad_qkv = dot(h_all, flat, TN)
    w_wide = w_qkv.astype(F32)
    by_row = (grad_qkv - shift[0][:, None] * sums_qkv) / gain[0][:, None]
    d_gain0 = jnp.sum(w_wide * by_row, axis=1)
    d_shift0 = jnp.sum(w_wide * sums_qkv, axis=1)
    up_sum = column_sum(g_pre).reshape(chips, 1, seq * ff_shard)
    up_sum = jnp.where(jnp.arange(2)[None, :, None] == core, up_sum, 0.0)
    vectors = jnp.stack(
        [
            d_gain0,
            d_gain1,
            d_gain2,
            d_shift0,
            d_shift1,
            d_shift2,
            spread_heads(sums_qkv[:lanes]),
            spread_heads(sums_qkv[2 * lanes :]),
            column_sum(g_one),
            spread(column_sum(dq_cross)),
            spread(column_sum(dkv_cross[:, half:])),
            column_sum(g_two),
            column_sum(cot_wide),
        ]
    )
    small = jnp.concatenate([vectors.T, up_sum.reshape(width, ff_shard // shard)], axis=1)
    small = jnp.pad(small, ((0, 0), (0, side - small.shape[1])))
    parts = jnp.concatenate([grad_qkv.astype(BF16), small.astype(BF16)], axis=1)
    parts = ring_scatter(net, parts.reshape(chips, 2, seq * shard, 3 * lanes + side))
    parts = parts.reshape(2, seq, shard, 3 * lanes + side)
    low = parts.astype(BF16)
    piece = jnp.zeros((2, seq, shard, 3 * lanes), BF16)
    piece = put(piece, pick(low, z, 1)[..., : 3 * lanes], z, 1)
    small = pick(parts, z, 1)[..., 3 * lanes :]
    for s in range(1, seq):
        got = net.along(pick(low, net.z_at(s), 1), s)
        piece = put(piece, got[..., : 3 * lanes], net.z_at(-s), 1)
        small += got[..., 3 * lanes :].astype(F32)
    own, other = own_first(net, piece)
    piece = by_core(net, own, net.sibling(other))
    sum_self = piece.reshape(2, seq, shard, 3, lanes).transpose(3, 2, 1, 0, 4)
    sum_self = sum_self.reshape(3, shard, width).astype(F32)
    own, other = own_first(net, small)
    small = own + net.sibling(other)
    vectors = small[:, :13].T
    return (
        layer_rows[None],
        token_grad[None],
        grad_memory[None],
        vectors[0:3],
        vectors[3:6],
        sum_self,
        sum_outs[:, :width],
        sum_cross,
        sum_outs[:, width:],
        sum_up,
        sum_down,
        vectors[6:13],
        small[:, 13 : 13 + ff_shard // shard].reshape(ff_shard),
    )


def solution(mesh):
    weight = P(AXES, None)
    return jax.shard_map(
        functools.partial(on_device, mesh=mesh),
        mesh=mesh,
        in_specs=(
            P("page", "seq", None),
            P("page", "seq", None),
            P("page", "seq", None),
            P("page"),
            P(None, AXES),
            P(None, AXES),
            P(None, AXES, None),
            weight,
            P(None, AXES, None),
            weight,
            weight,
            weight,
            P(None, AXES),
            P(AXES),
        ),
        out_specs=(
            P("page", "seq", None),
            P("page", "seq", None),
            P("page", "seq", None),
            P(None, AXES),
            P(None, AXES),
            P(None, AXES, None),
            weight,
            P(None, AXES, None),
            weight,
            weight,
            weight,
            P(None, AXES),
            P(AXES),
        ),
        check_vma=False,
    )
```
